512 devices in a mesh: elem: 32 (over x, y_lo, core), basis: 16 (over z, y_hi).
Axes of the slice: x: 4, y: 8 (y_hi: 2, y_lo: 4; y = y_hi * 4 + y_lo), z: 8, core: 2. Of those that a mesh axis runs over, the one named last changes fastest.
Arguments:
- basis_vals: bfloat16 [64, 60, 46656], P('elem', None, 'basis'), may hold values from -6 to 6
- basis_grad: bfloat16 [64, 3, 60, 46656], P('elem', None, None, 'basis'), may hold values from -6 to 6
- potential: float32 [64, 46656], P('elem', 'basis'), may hold values from -12 to 12
- face_traces: bfloat16 [64, 2, 2, 60, 1296], P('elem', None, None, None, 'basis'), may hold values from -6 to 6
- penalty: float32 [64], replicated, may hold values from 4 to 40
- orientation: int32 [64], replicated, may hold values from 0 to 1
Outputs:
- blocks: float32 [64, 2, 3600], P('elem', None, 'basis')
The draws below stay inside these ranges and needn't reach their ends.
All inputs are finite; a program needn't handle non-finite values.
Results may differ from the reference program's by a relative error of at most 0.0003.
Values may be sent and summed in bfloat16 or wider, within the bound.
No kernel may reach another device: no remote copies, remote signals or barrier semaphores. Data moves between devices by JAX's collectives and lax.ppermute only.
A program may use at most 64 MiB of HBM per device.

```python
import math
import jax
import jax.numpy as jnp
from jax import lax

NB = 60
PTS = 46656
FP = 1296
E = 64


def place_ends(result, own_key, smallest, top_value):
    extent = result.shape
    index_at = [jax.random.randint(jax.random.fold_in(own_key, axis), (), 0, extent[axis]) for axis in range(len(extent))]
    result = result.at[tuple(index_at)].set(smallest)
    longest = extent.index(max(extent))
    index_at[longest] = (index_at[longest] + 1) % extent[longest]
    return result.at[tuple(index_at)].set(top_value)


def shard_levels(stream_key, dims, split, smallest, high):
    def one(axis_at, shards_of):
        draws = jax.random.uniform(jax.random.fold_in(jax.random.fold_in(stream_key, 6), axis_at), (shards_of,), jnp.float32, smallest / len(split), high / len(split))
        return jnp.repeat(jnp.exp(draws), dims[axis_at] // shards_of).reshape((-1,) + (1,) * (len(dims) - axis_at - 1))

    gain = one(*split[0])
    for cut in split[1:]:
        gain = gain * one(*cut)
    return gain


def centred(rng, dims, scale, limit, shards=(), kind=jnp.bfloat16):
    level = shard_levels(rng, dims, shards, -0.22, 0.18) if shards else 1.0
    result = jax.random.normal(rng, dims, jnp.float32) * scale * level
    return jnp.minimum(jnp.maximum(result, -limit), limit).astype(kind)


def setup_inputs(seed: int = 0) -> dict:
    splits = jax.random.split(jax.random.key(seed), 7)
    basis_vals = centred(splits[0], (E, NB, PTS), 1.0, 6.0, ((0, 32), (2, 16)))
    basis_grad = centred(splits[1], (E, 3, NB, PTS), 1.0, 6.0, ((0, 32), (3, 16)))
    potential = centred(splits[2], (E, PTS), 2.0, 12.0, ((0, 32), (1, 16)), jnp.float32)
    face_traces = centred(splits[3], (E, 2, 2, NB, FP), 1.0, 6.0, ((0, 32), (4, 16)))
    penalty = jnp.clip(jnp.exp(jax.random.uniform(splits[4], (E,), jnp.float32, math.log(4.0), math.log(40.0))), 4.0, 40.0)
    orientation = place_ends(jax.random.randint(splits[5], (E,), 0, 2), jax.random.fold_in(splits[5], 1), 0, 1).astype(jnp.int32)
    return dict(basis_vals=basis_vals, basis_grad=basis_grad, potential=potential, face_traces=face_traces, penalty=penalty, orientation=orientation)


def orient(face_traces, codes):
    flag = (codes == 0)[:, None, None, None]
    upper = jnp.where(flag, face_traces[:, 1], face_traces[:, 0])
    lower = jnp.where(flag, face_traces[:, 0], face_traces[:, 1])
    sign = (1 - 2 * codes).astype(jnp.bfloat16)[:, None, None]
    return upper[:, 0], upper[:, 1] * sign, lower[:, 0], lower[:, 1] * sign


def face_gram(left, right):
    return jnp.einsum("eaq,ebq->eab", left.astype(jnp.float32), right.astype(jnp.float32))


def element_volume(item):
    values, grads, pot = item
    weighted = (values.astype(jnp.float32) * pot[None, :] * (1.0 / PTS)).astype(jnp.bfloat16)
    total = jnp.dot(weighted, values.T, preferred_element_type=jnp.float32)
    kinetic = jnp.zeros((NB, NB), jnp.float32)
    for comp in range(3):
        kinetic = kinetic + jnp.dot(grads[comp], grads[comp].T, preferred_element_type=jnp.float32)
    return total + (0.5 / PTS) * kinetic


def reference(basis_vals, basis_grad, potential, face_traces, penalty, orientation):
    volume = lax.map(element_volume, (basis_vals, basis_grad, potential))
    vp, dp, vm, dm = orient(face_traces, orientation)
    upper_pen = 0.5 * (penalty + jnp.roll(penalty, -1))
    lower_pen = 0.5 * (jnp.roll(penalty, 1) + penalty)
    own = (-0.25 * (face_gram(dp, vp) + face_gram(vp, dp)) + upper_pen[:, None, None] * face_gram(vp, vp)
           + 0.25 * (face_gram(dm, vm) + face_gram(vm, dm)) + lower_pen[:, None, None] * face_gram(vm, vm))
    diag = volume + own * (1.0 / FP)
    diag = 0.5 * (diag + jnp.swapaxes(diag, 1, 2))
    vm_next = jnp.roll(vm, -1, axis=0)
    dm_next = jnp.roll(dm, -1, axis=0)
    pair = (0.25 * (face_gram(dp, vm_next) - face_gram(vp, dm_next))
            - upper_pen[:, None, None] * face_gram(vp, vm_next)) * (1.0 / FP)
    count = diag.shape[0]
    return jnp.stack([diag.reshape(count, NB * NB), pair.reshape(count, NB * NB)], axis=1)
```

```python
import jax
import jax.numpy as jnp
from jax import lax
from jax.experimental import pallas as pl
from jax.experimental.pallas import tpu as pltpu
from jax.sharding import PartitionSpec as P

PTS = 46656
FP = 1296
LANES = 128
NT = (((1,), (1,)), ((), ()))
MIB = 1024 * 1024


def gram(left, right):
    return lax.dot_general(left, right, NT, preferred_element_type=jnp.float32)


def merged(value):
    rows, pair, lanes = value.shape
    return value.reshape(rows * pair, lanes)


def parities(size):
    shape = (size, size)
    row = lax.broadcasted_iota(jnp.int32, shape, 0) % 2
    col = lax.broadcasted_iota(jnp.int32, shape, 1) % 2
    return row, col


def fold(first, second, stage, turned, width):
    size = first.shape[0]
    half = size // 2
    stage[0] = first
    stage[1] = second
    rows = [stage[n, pl.ds(0, half, stride=2), :] + stage[n, pl.ds(1, half, stride=2), :] for n in range(2)]
    turned[...] = jnp.concatenate(rows, axis=0).T
    both = turned[pl.ds(0, half, stride=2), :] + turned[pl.ds(1, half, stride=2), :]
    return both[:width, :width], both[:width, half : half + width]


def local_terms(grad, vals, pot, faces, penalty, orientation, diag, cross, scales, edge, grads, tiles, pots, sides,
                pens, codes, stage, turned, sems):
    comps, width, count, points = grad.shape
    even = points // LANES * LANES
    rows = width * count

    moves = [
        pltpu.make_async_copy(source, target, sems.at[comps + n])
        for n, (source, target) in enumerate(
            ((penalty, pens), (orientation, codes), (faces, sides), (pot, pots), (vals, tiles))
        )
    ]

    def grad_move(comp):
        return pltpu.make_async_copy(grad.at[comp], grads.at[comp], sems.at[comp])

    for move in moves:
        move.start()
    for comp in range(comps):
        grad_move(comp).start()
    for move in moves[:3]:
        move.wait()

    first = lax.axis_index("elem") * count
    total = penalty.shape[0]
    row, col = parities(rows)

    def code_at(element):
        return codes[lax.rem(first + element, total)]

    def sign_of(code):
        return (1 - 2 * code).astype(jnp.float32)

    def pen_between(element):
        left = pens[lax.rem(first + element + total - 1, total)]
        return 0.5 * (left + pens[lax.rem(first + element, total)])

    uppers = [merged(sides[element, 1 - code_at(element)]) for element in range(count)]
    lowers = [merged(sides[element, code_at(element)]) for element in range(count)]

    def face_part(element):
        mixed = jnp.where(row != col, 0.25 * sign_of(code_at(element)), 0.0)
        both = row + col == 0
        upper_scale = jnp.where(both, pen_between(element + 1), -mixed)
        lower_scale = jnp.where(both, pen_between(element), mixed)
        upper, lower = uppers[element], lowers[element]
        return (upper_scale * gram(upper, upper) + lower_scale * gram(lower, lower)) * (1.0 / FP)

    def cross_scale(element):
        upper_sign, lower_sign = sign_of(code_at(element)), sign_of(code_at(element + 1))
        return (1.0 / FP) * jnp.where(
            row == 0,
            jnp.where(col == 0, -pen_between(element + 1), 0.25 * upper_sign),
            jnp.where(col == 0, -0.25 * lower_sign, 0.0),
        )

    cross[...] = cross_scale(0) * gram(lowers[1], uppers[0])
    edge[...] = uppers[count - 1]
    scale = cross_scale(count - 1)
    for side in range(2):
        scales[side] = jnp.where(code_at(count) == side, scale, 0.0)
    face_parts = [face_part(element) for element in range(count)]

    for move in moves[3:]:
        move.wait()
    odd = lax.broadcasted_iota(jnp.int32, (rows, LANES), 0) % 2 == 1

    def weighted(tile, level):
        level = jnp.where(odd[:, : tile.shape[1]], level[1:2], level[0:1])
        return (tile.astype(jnp.float32) * level * (1.0 / PTS)).astype(jnp.bfloat16)

    tile = merged(tiles[:, :, :even])
    parts = [weighted(tile[:, at : at + LANES], pots[:, at : at + LANES]) for at in range(0, even, LANES)]
    end = merged(tiles[:, :, even:])
    volume = gram(jnp.concatenate(parts, axis=1), tile) + gram(weighted(end, pots[:, even:]), end)

    def add_comp(comp, kinetic):
        grad_move(comp).wait()
        slope = merged(grads[comp, :, :, :even])
        end = merged(grads[comp, :, :, even:])
        return kinetic + gram(slope, slope) + gram(end, end)

    kinetic = lax.fori_loop(0, comps, add_comp, jnp.zeros((rows, rows), jnp.float32))
    inner = 0.5 * (volume + volume.T) + (0.5 / PTS) * kinetic
    parts = [
        jnp.where((row == element) & (col == element), inner, 0.0) + face_parts[element] for element in range(count)
    ]
    diag[0], diag[1] = fold(*parts, stage, turned, width)


def pair_terms(arrived, edge, cross, scales, diag, out, stage, turned, rows):
    width = diag.shape[1]
    share = out.shape[2]
    upper = edge[...]
    parts = [gram(merged(arrived[0, side]), upper) * scales[side] for side in range(2)]
    pairs = fold(cross[...], parts[0] + parts[1], stage, turned, width)
    kinds = 2 * len(pairs)
    for element, pair in enumerate(pairs):
        rows[pl.ds(2 * element, width, stride=kinds), :] = diag[element]
        rows[pl.ds(2 * element + 1, width, stride=kinds), :] = pair
    for slot, owner in enumerate(exchange_order(out.shape[0])):
        at, end = owner * share, (owner + 1) * share
        pieces = []
        while at < end:
            row, col = divmod(at, width)
            size = min(width - col, end - at)
            pieces.append(rows[pl.ds(kinds * row, kinds), pl.ds(col, size)])
            at += size
        out[slot] = jnp.concatenate(pieces, axis=1)


def exchange_order(ways):
    return [(slot + ways * 11 // 16) % ways for slot in range(ways)]


def total_terms(shared, out):
    total = jnp.sum(shared[...], axis=0)
    for element in range(out.shape[0]):
        out[element] = total[2 * element : 2 * element + 2]


def from_behind(value, axis, steps):
    count = lax.axis_size(axis)
    pairs = [(source, (source + steps) % count) for source in range(count)]
    return lax.ppermute(value, axis, pairs)


def on_device(basis_vals, basis_grad, potential, face_traces, penalty, orientation):
    count, width, points = basis_vals.shape
    comps = basis_grad.shape[1]
    face_points = face_traces.shape[-1]
    faces = face_traces.transpose(0, 1, 3, 2, 4)
    arrived = from_behind(faces, "elem", -1)
    grad = basis_grad.transpose(1, 2, 0, 3)
    vals = basis_vals.transpose(1, 0, 2)
    held = (grad, vals, potential, faces, penalty, orientation)
    held = [pltpu.with_memory_space_constraint(array, pltpu.HBM) for array in held]
    rows = width * count
    any_space = pl.BlockSpec(memory_space=pl.ANY)
    in_vmem = pl.BlockSpec(memory_space=pltpu.VMEM)
    fold_scratch = [pltpu.VMEM((2, rows, rows), jnp.float32), pltpu.VMEM((rows, rows), jnp.float32)]
    diag, cross, scales, edge = pl.pallas_call(
        local_terms,
        out_shape=[
            pltpu.VMEM((count, width, width), jnp.float32),
            pltpu.VMEM((rows, rows), jnp.float32),
            pltpu.VMEM((2, rows, rows), jnp.float32),
            pltpu.VMEM((rows, face_points), jnp.bfloat16),
        ],
        in_specs=[any_space] * 6,
        out_specs=[in_vmem] * 4,
        scratch_shapes=[
            pltpu.VMEM(grad.shape, jnp.bfloat16),
            pltpu.VMEM(vals.shape, jnp.bfloat16),
            pltpu.VMEM(potential.shape, jnp.float32),
            pltpu.VMEM(faces.shape, jnp.bfloat16),
            pltpu.SMEM(penalty.shape, jnp.float32),
            pltpu.SMEM(orientation.shape, jnp.int32),
            *fold_scratch,
            pltpu.SemaphoreType.DMA((comps + 5,)),
        ],
        compiler_params=pltpu.CompilerParams(vmem_limit_bytes=16 * MIB),
        cost_estimate=pl.CostEstimate(flops=400_000_000, bytes_accessed=3_000_000, transcendentals=0),
        name="local_terms",
    )(*held)
    ways = lax.axis_size("basis")
    share = width * width // ways
    terms = pl.pallas_call(
        pair_terms,
        out_shape=pltpu.VMEM((ways, 2 * count, share), jnp.float32),
        in_specs=[in_vmem] * 5,
        out_specs=in_vmem,
        scratch_shapes=[*fold_scratch, pltpu.VMEM((2 * count * width, width), jnp.float32)],
        compiler_params=pltpu.CompilerParams(vmem_limit_bytes=8 * MIB),
        name="pair_terms",
    )(pltpu.with_memory_space_constraint(arrived, pltpu.VMEM), edge, cross, scales, diag)
    shared = lax.all_to_all(terms, "basis", 0, 0, axis_index_groups=[exchange_order(ways)])
    return pl.pallas_call(
        total_terms,
        out_shape=jax.ShapeDtypeStruct((count, 2, share), jnp.float32),
        in_specs=[in_vmem],
        out_specs=in_vmem,
        compiler_params=pltpu.CompilerParams(vmem_limit_bytes=8 * MIB),
        name="total_terms",
    )(pltpu.with_memory_space_constraint(shared, pltpu.VMEM))


def solution(mesh):
    in_specs = (
        P("elem", None, "basis"),
        P("elem", None, None, "basis"),
        P("elem", "basis"),
        P("elem", None, None, None, "basis"),
        P(),
        P(),
    )
    out_specs = P("elem", None, "basis")
    return jax.shard_map(
        on_device, mesh=mesh, in_specs=in_specs, out_specs=out_specs, check_vma=False
    )
```

```python
import jax
import jax.numpy as jnp
from jax import lax
from jax.experimental import pallas as pl
from jax.experimental.pallas import tpu as pltpu
from jax.sharding import PartitionSpec as P

PTS = 46656
FP = 1296
LANES = 128
NT = (((1,), (1,)), ((), ()))
MIB = 1024 * 1024


def gram(left, right):
    return lax.dot_general(left, right, NT, preferred_element_type=jnp.float32)


def merged(value):
    rows, pair, lanes = value.shape
    return value.reshape(rows * pair, lanes)


def parities(size):
    shape = (size, size)
    row = lax.broadcasted_iota(jnp.int32, shape, 0) % 2
    col = lax.broadcasted_iota(jnp.int32, shape, 1) % 2
    return row, col


def fold(first, second, stage, turned, width):
    size = first.shape[0]
    half = size // 2
    stage[0] = first
    stage[1] = second
    rows = [stage[n, pl.ds(0, half, stride=2), :] + stage[n, pl.ds(1, half, stride=2), :] for n in range(2)]
    turned[...] = jnp.concatenate(rows, axis=0).T
    both = turned[pl.ds(0, half, stride=2), :] + turned[pl.ds(1, half, stride=2), :]
    return both[:width, :width], both[:width, half : half + width]


def local_terms(grad, vals, pot, faces, penalty, orientation, diag, cross, scales, edge, grads, tiles, pots, sides,
                pens, codes, stage, turned, sems):
    comps, width, count, points = grad.shape
    rows = width * count

    moves = [
        pltpu.make_async_copy(source, target, sems.at[comps + n])
        for n, (source, target) in enumerate(
            ((penalty, pens), (orientation, codes), (faces, sides), (pot, pots), (vals, tiles))
        )
    ]

    def grad_move(comp):
        return pltpu.make_async_copy(grad.at[comp], grads.at[comp], sems.at[comp])

    for move in moves[:3]:
        move.start()
    grad_move(0).start()
    for move in moves[3:]:
        move.start()
    for comp in range(1, comps):
        grad_move(comp).start()
    for move in moves[:3]:
        move.wait()

    first = lax.axis_index("elem") * count
    total = penalty.shape[0]
    row, col = parities(rows)

    def code_at(element):
        return codes[lax.rem(first + element, total)]

    def sign_of(code):
        return (1 - 2 * code).astype(jnp.float32)

    def pen_between(element):
        left = pens[lax.rem(first + element + total - 1, total)]
        return 0.5 * (left + pens[lax.rem(first + element, total)])

    uppers = [merged(sides[element, 1 - code_at(element)]) for element in range(count)]
    lowers = [merged(sides[element, code_at(element)]) for element in range(count)]

    def face_part(element):
        mixed = jnp.where(row != col, 0.25 * sign_of(code_at(element)), 0.0)
        both = row + col == 0
        upper_scale = jnp.where(both, pen_between(element + 1), -mixed)
        lower_scale = jnp.where(both, pen_between(element), mixed)
        upper, lower = uppers[element], lowers[element]
        return (upper_scale * gram(upper, upper) + lower_scale * gram(lower, lower)) * (1.0 / FP)

    def cross_scale(element):
        upper_sign, lower_sign = sign_of(code_at(element)), sign_of(code_at(element + 1))
        return (1.0 / FP) * jnp.where(
            row == 0,
            jnp.where(col == 0, -pen_between(element + 1), 0.25 * upper_sign),
            jnp.where(col == 0, -0.25 * lower_sign, 0.0),
        )

    cross[...] = cross_scale(0) * gram(lowers[1], uppers[0])
    edge[...] = uppers[count - 1]
    scale = cross_scale(count - 1)
    for side in range(2):
        scales[side] = jnp.where(code_at(count) == side, scale, 0.0)
    face_parts = [face_part(element) for element in range(count)]

    odd = lax.broadcasted_iota(jnp.int32, (rows, LANES), 0) % 2 == 1

    def weighted(tile, level):
        level = jnp.where(odd[:, : tile.shape[1]], level[1:2], level[0:1])
        return (tile.astype(jnp.float32) * level * (1.0 / PTS)).astype(jnp.bfloat16)

    volume, kinetic = [], []
    half = points // LANES // 2 * LANES
    spans = ((0, half), (half, points))
    for comp in range(comps):
        grad_move(comp).wait()
        for at, end in spans:
            slope = merged(grads[comp, :, :, at:end])
            kinetic.append(gram(slope, slope))
        if comp == 0:
            for move in moves[3:]:
                move.wait()
            for at, end in spans:
                tile = merged(tiles[:, :, at:end])
                parts = [
                    weighted(tile[:, n - at : min(n + LANES, end) - at], pots[:, n : min(n + LANES, end)])
                    for n in range(at, end, LANES)
                ]
                volume.append(gram(jnp.concatenate(parts, axis=1), tile))
    volume, kinetic = sum(volume), sum(kinetic)
    inner = 0.5 * (volume + volume.T) + (0.5 / PTS) * kinetic
    parts = [
        jnp.where((row == element) & (col == element), inner, 0.0) + face_parts[element] for element in range(count)
    ]
    diag[0], diag[1] = fold(*parts, stage, turned, width)


def pair_terms(arrived, edge, cross, scales, diag, out, stage, turned, rows):
    width = diag.shape[1]
    share = out.shape[2]
    upper = edge[...]
    parts = [gram(merged(arrived[0, side]), upper) * scales[side] for side in range(2)]
    pairs = fold(cross[...], parts[0] + parts[1], stage, turned, width)
    kinds = 2 * len(pairs)
    for element, pair in enumerate(pairs):
        rows[pl.ds(2 * element, width, stride=kinds), :] = diag[element]
        rows[pl.ds(2 * element + 1, width, stride=kinds), :] = pair
    for slot, owner in enumerate(exchange_order(out.shape[0])):
        at, end = owner * share, (owner + 1) * share
        pieces = []
        while at < end:
            row, col = divmod(at, width)
            size = min(width - col, end - at)
            pieces.append(rows[pl.ds(kinds * row, kinds), pl.ds(col, size)])
            at += size
        out[slot] = jnp.concatenate(pieces, axis=1)


def exchange_order(ways):
    return [(slot + ways * 11 // 16) % ways for slot in range(ways)]


def total_terms(shared, out):
    total = jnp.sum(shared[...], axis=0)
    for element in range(out.shape[0]):
        out[element] = total[2 * element : 2 * element + 2]


def from_behind(value, axis, steps):
    count = lax.axis_size(axis)
    pairs = [(source, (source + steps) % count) for source in range(count)]
    return lax.ppermute(value, axis, pairs)


def on_device(basis_vals, basis_grad, potential, face_traces, penalty, orientation):
    count, width, points = basis_vals.shape
    comps = basis_grad.shape[1]
    face_points = face_traces.shape[-1]
    faces = face_traces.transpose(0, 1, 3, 2, 4)
    arrived = from_behind(faces, "elem", -1)
    grad = basis_grad.transpose(1, 2, 0, 3)
    vals = basis_vals.transpose(1, 0, 2)
    held = (grad, vals, potential, faces, penalty, orientation)
    held = [pltpu.with_memory_space_constraint(array, pltpu.HBM) for array in held]
    rows = width * count
    any_space = pl.BlockSpec(memory_space=pl.ANY)
    in_vmem = pl.BlockSpec(memory_space=pltpu.VMEM)
    fold_scratch = [pltpu.VMEM((2, rows, rows), jnp.float32), pltpu.VMEM((rows, rows), jnp.float32)]
    diag, cross, scales, edge = pl.pallas_call(
        local_terms,
        out_shape=[
            pltpu.VMEM((count, width, width), jnp.float32),
            pltpu.VMEM((rows, rows), jnp.float32),
            pltpu.VMEM((2, rows, rows), jnp.float32),
            pltpu.VMEM((rows, face_points), jnp.bfloat16),
        ],
        in_specs=[any_space] * 6,
        out_specs=[in_vmem] * 4,
        scratch_shapes=[
            pltpu.VMEM(grad.shape, jnp.bfloat16),
            pltpu.VMEM(vals.shape, jnp.bfloat16),
            pltpu.VMEM(potential.shape, jnp.float32),
            pltpu.VMEM(faces.shape, jnp.bfloat16),
            pltpu.SMEM(penalty.shape, jnp.float32),
            pltpu.SMEM(orientation.shape, jnp.int32),
            *fold_scratch,
            pltpu.SemaphoreType.DMA((comps + 5,)),
        ],
        compiler_params=pltpu.CompilerParams(vmem_limit_bytes=16 * MIB),
        cost_estimate=pl.CostEstimate(flops=400_000_000, bytes_accessed=3_000_000, transcendentals=0),
        name="local_terms",
    )(*held)
    ways = lax.axis_size("basis")
    share = width * width // ways
    terms = pl.pallas_call(
        pair_terms,
        out_shape=pltpu.VMEM((ways, 2 * count, share), jnp.float32),
        in_specs=[in_vmem] * 5,
        out_specs=in_vmem,
        scratch_shapes=[*fold_scratch, pltpu.VMEM((2 * count * width, width), jnp.float32)],
        compiler_params=pltpu.CompilerParams(vmem_limit_bytes=8 * MIB),
        name="pair_terms",
    )(pltpu.with_memory_space_constraint(arrived, pltpu.VMEM), edge, cross, scales, diag)
    shared = lax.all_to_all(terms, "basis", 0, 0, axis_index_groups=[exchange_order(ways)])
    return pl.pallas_call(
        total_terms,
        out_shape=jax.ShapeDtypeStruct((count, 2, share), jnp.float32),
        in_specs=[in_vmem],
        out_specs=in_vmem,
        compiler_params=pltpu.CompilerParams(vmem_limit_bytes=8 * MIB),
        name="total_terms",
    )(pltpu.with_memory_space_constraint(shared, pltpu.VMEM))


def solution(mesh):
    in_specs = (
        P("elem", None, "basis"),
        P("elem", None, None, "basis"),
        P("elem", "basis"),
        P("elem", None, None, None, "basis"),
        P(),
        P(),
    )
    out_specs = P("elem", None, "basis")
    return jax.shard_map(
        on_device, mesh=mesh, in_specs=in_specs, out_specs=out_specs, check_vma=False
    )
```

```python
import jax
import jax.numpy as jnp
from jax import lax
from jax.experimental import pallas as pl
from jax.experimental.pallas import tpu as pltpu
from jax.sharding import PartitionSpec as P

PTS = 46656
FP = 1296
LANES = 128
NT = (((1,), (1,)), ((), ()))
MIB = 1024 * 1024


def gram(left, right):
    return lax.dot_general(left, right, NT, preferred_element_type=jnp.float32)


def merged(array):
    *lead, rows, pair, lanes = array.shape
    return array.reshape(*lead, rows * pair, lanes)


def parities(size):
    shape = (size, size)
    row = lax.broadcasted_iota(jnp.int32, shape, 0) % 2
    col = lax.broadcasted_iota(jnp.int32, shape, 1) % 2
    return row, col


def fold(first, second, stage, turned, width):
    size = first.shape[0]
    half = size // 2
    stage[0] = first
    stage[1] = second
    rows = [stage[n, pl.ds(0, half, stride=2), :] + stage[n, pl.ds(1, half, stride=2), :] for n in range(2)]
    turned[...] = jnp.concatenate(rows, axis=0).T
    both = turned[pl.ds(0, half, stride=2), :] + turned[pl.ds(1, half, stride=2), :]
    return both[:width, :width], both[:width, half : half + width]


def local_terms(grad, vals, pot, faces, penalty, orientation, diag, cross, scales, edge, grads, tiles, pots, sides,
                pens, codes, stage, turned, sems):
    comps, width, count, points = grad.shape
    even = points // LANES * LANES
    rows = width * count

    moves = [
        pltpu.make_async_copy(source, target, sems.at[comps + n])
        for n, (source, target) in enumerate(
            ((penalty, pens), (orientation, codes), (merged(faces), sides), (pot, pots), (merged(vals), tiles))
        )
    ]

    def grad_move(comp):
        return pltpu.make_async_copy(merged(grad).at[comp], grads.at[comp], sems.at[comp])

    for move in moves:
        move.start()
    for comp in range(comps):
        grad_move(comp).start()
    for move in moves[:3]:
        move.wait()

    first = lax.axis_index("elem") * count
    total = penalty.shape[0]
    row, col = parities(rows)

    def code_at(element):
        return codes[lax.rem(first + element, total)]

    def sign_of(code):
        return (1 - 2 * code).astype(jnp.float32)

    def pen_between(element):
        left = pens[lax.rem(first + element + total - 1, total)]
        return 0.5 * (left + pens[lax.rem(first + element, total)])

    uppers = [sides[element, 1 - code_at(element)] for element in range(count)]
    lowers = [sides[element, code_at(element)] for element in range(count)]

    def face_part(element):
        mixed = jnp.where(row != col, 0.25 * sign_of(code_at(element)), 0.0)
        both = row + col == 0
        upper_scale = jnp.where(both, pen_between(element + 1), -mixed)
        lower_scale = jnp.where(both, pen_between(element), mixed)
        upper, lower = uppers[element], lowers[element]
        return (upper_scale * gram(upper, upper) + lower_scale * gram(lower, lower)) * (1.0 / FP)

    def cross_scale(element):
        upper_sign, lower_sign = sign_of(code_at(element)), sign_of(code_at(element + 1))
        return (1.0 / FP) * jnp.where(
            row == 0,
            jnp.where(col == 0, -pen_between(element + 1), 0.25 * upper_sign),
            jnp.where(col == 0, -0.25 * lower_sign, 0.0),
        )

    cross[...] = cross_scale(0) * gram(lowers[1], uppers[0])
    edge[...] = uppers[count - 1]
    scale = cross_scale(count - 1)
    for side in range(2):
        scales[side] = jnp.where(code_at(count) == side, scale, 0.0)
    face_parts = [face_part(element) for element in range(count)]

    for move in moves[3:]:
        move.wait()
    odd = lax.broadcasted_iota(jnp.int32, (rows, LANES), 0) % 2 == 1

    def weighted(tile, level):
        level = jnp.where(odd[:, : tile.shape[1]], level[1:2], level[0:1])
        return (tile.astype(jnp.float32) * level * (1.0 / PTS)).astype(jnp.bfloat16)

    tile = tiles[:, :even]
    parts = [weighted(tile[:, at : at + LANES], pots[:, at : at + LANES]) for at in range(0, even, LANES)]
    end = tiles[:, even:]
    volume = gram(jnp.concatenate(parts, axis=1), tile) + gram(weighted(end, pots[:, even:]), end)

    def add_comp(comp, kinetic):
        grad_move(comp).wait()
        slope = grads[comp, :, :even]
        end = grads[comp, :, even:]
        return kinetic + gram(slope, slope) + gram(end, end)

    kinetic = lax.fori_loop(0, comps, add_comp, jnp.zeros((rows, rows), jnp.float32))
    inner = 0.5 * (volume + volume.T) + (0.5 / PTS) * kinetic
    parts = [
        jnp.where((row == element) & (col == element), inner, 0.0) + face_parts[element] for element in range(count)
    ]
    diag[0], diag[1] = fold(*parts, stage, turned, width)


def pair_terms(arrived, edge, cross, scales, diag, out, stage, turned, rows):
    width = diag.shape[1]
    share = out.shape[2]
    upper = edge[...]
    parts = [gram(merged(arrived[0, side]), upper) * scales[side] for side in range(2)]
    pairs = fold(cross[...], parts[0] + parts[1], stage, turned, width)
    kinds = 2 * len(pairs)
    for element, pair in enumerate(pairs):
        rows[pl.ds(2 * element, width, stride=kinds), :] = diag[element]
        rows[pl.ds(2 * element + 1, width, stride=kinds), :] = pair
    ways = out.shape[0] // 2
    start = own_slots(ways)
    slots = [exchange_order(ways).index(owner) for owner in range(ways)]
    out[pl.ds(ways - start, ways)] = jnp.zeros((ways, kinds, share), jnp.float32)
    for owner in range(ways):
        at, end = owner * share, (owner + 1) * share
        pieces = []
        while at < end:
            row, col = divmod(at, width)
            size = min(width - col, end - at)
            pieces.append(rows[pl.ds(kinds * row, kinds), pl.ds(col, size)])
            at += size
        out[start + slots[owner]] = jnp.concatenate(pieces, axis=1)


def own_slots(ways):
    return ways * (lax.rem(lax.axis_index("elem") // 2, 4) // 2)


def exchange_order(ways):
    rings = max(ways // 2, 1)
    root = 2 * (5 * rings // 8) + 1 if ways > 1 else 0

    def hops(share):
        step = (share // 2 - root // 2) % rings
        return min(step, rings - step) + 4 * ((share ^ root) & 1)

    return [root] + sorted((share for share in range(ways) if share != root), key=hops, reverse=True)


def exchange_groups(elems, ways):
    order = exchange_order(ways)
    return [
        [row * ways + share for row in (elem, elem + 4) for share in order]
        for elem in range(elems)
        if (elem // 2) % 4 < 2
    ]


def total_terms(shared, out):
    ways = shared.shape[0] // 2
    total = jnp.sum(shared[pl.ds(own_slots(ways), ways)], axis=0)
    for element in range(out.shape[0]):
        out[element] = total[2 * element : 2 * element + 2]


def from_behind(value, axis, steps):
    count = lax.axis_size(axis)
    pairs = [(source, (source + steps) % count) for source in range(count)]
    return lax.ppermute(value, axis, pairs)


def on_device(basis_vals, basis_grad, potential, face_traces, penalty, orientation):
    count, width, points = basis_vals.shape
    comps = basis_grad.shape[1]
    face_points = face_traces.shape[-1]
    faces = face_traces.transpose(0, 1, 3, 2, 4)
    arrived = from_behind(faces, "elem", -1)
    grad = basis_grad.transpose(1, 2, 0, 3)
    vals = basis_vals.transpose(1, 0, 2)
    held = (grad, vals, potential, faces, penalty, orientation)
    held = [pltpu.with_memory_space_constraint(array, pltpu.HBM) for array in held]
    rows = width * count
    any_space = pl.BlockSpec(memory_space=pl.ANY)
    in_vmem = pl.BlockSpec(memory_space=pltpu.VMEM)
    fold_scratch = [pltpu.VMEM((2, rows, rows), jnp.float32), pltpu.VMEM((rows, rows), jnp.float32)]
    diag, cross, scales, edge = pl.pallas_call(
        local_terms,
        out_shape=[
            pltpu.VMEM((count, width, width), jnp.float32),
            pltpu.VMEM((rows, rows), jnp.float32),
            pltpu.VMEM((2, rows, rows), jnp.float32),
            pltpu.VMEM((rows, face_points), jnp.bfloat16),
        ],
        in_specs=[any_space] * 6,
        out_specs=[in_vmem] * 4,
        scratch_shapes=[
            pltpu.VMEM((comps, rows, points), jnp.bfloat16),
            pltpu.VMEM((rows, points), jnp.bfloat16),
            pltpu.VMEM(potential.shape, jnp.float32),
            pltpu.VMEM((count, 2, rows, face_points), jnp.bfloat16),
            pltpu.SMEM(penalty.shape, jnp.float32),
            pltpu.SMEM(orientation.shape, jnp.int32),
            *fold_scratch,
            pltpu.SemaphoreType.DMA((comps + 5,)),
        ],
        compiler_params=pltpu.CompilerParams(vmem_limit_bytes=16 * MIB),
        cost_estimate=pl.CostEstimate(flops=400_000_000, bytes_accessed=3_000_000, transcendentals=0),
        name="local_terms",
    )(*held)
    ways = lax.axis_size("basis")
    share = width * width // ways
    terms = pl.pallas_call(
        pair_terms,
        out_shape=pltpu.VMEM((2 * ways, 2 * count, share), jnp.float32),
        in_specs=[in_vmem] * 5,
        out_specs=in_vmem,
        scratch_shapes=[*fold_scratch, pltpu.VMEM((2 * count * width, width), jnp.float32)],
        compiler_params=pltpu.CompilerParams(vmem_limit_bytes=8 * MIB),
        name="pair_terms",
    )(pltpu.with_memory_space_constraint(arrived, pltpu.VMEM), edge, cross, scales, diag)
    groups = exchange_groups(lax.axis_size("elem"), ways)
    shared = lax.all_to_all(terms, ("elem", "basis"), 0, 0, axis_index_groups=groups)
    return pl.pallas_call(
        total_terms,
        out_shape=jax.ShapeDtypeStruct((count, 2, share), jnp.float32),
        in_specs=[in_vmem],
        out_specs=in_vmem,
        compiler_params=pltpu.CompilerParams(vmem_limit_bytes=8 * MIB),
        name="total_terms",
    )(pltpu.with_memory_space_constraint(shared, pltpu.VMEM))


def solution(mesh):
    in_specs = (
        P("elem", None, "basis"),
        P("elem", None, None, "basis"),
        P("elem", "basis"),
        P("elem", None, None, None, "basis"),
        P(),
        P(),
    )
    out_specs = P("elem", None, "basis")
    return jax.shard_map(
        on_device, mesh=mesh, in_specs=in_specs, out_specs=out_specs, check_vma=False
    )
```

```python
import jax
import jax.numpy as jnp
from jax import lax
from jax.experimental import pallas as pl
from jax.experimental.pallas import tpu as pltpu
from jax.sharding import PartitionSpec as P

PTS = 46656
FP = 1296
LANES = 128
NT = (((1,), (1,)), ((), ()))
MIB = 1024 * 1024


def gram(left, right):
    return lax.dot_general(left, right, NT, preferred_element_type=jnp.float32)


def merged(array):
    *lead, rows, pair, lanes = array.shape
    return array.reshape(*lead, rows * pair, lanes)


def parities(size):
    shape = (size, size)
    row = lax.broadcasted_iota(jnp.int32, shape, 0) % 2
    col = lax.broadcasted_iota(jnp.int32, shape, 1) % 2
    return row, col


def fold(first, second, stage, turned, width):
    size = first.shape[0]
    half = size // 2
    stage[0] = first
    stage[1] = second
    rows = [stage[n, pl.ds(0, half, stride=2), :] + stage[n, pl.ds(1, half, stride=2), :] for n in range(2)]
    turned[...] = jnp.concatenate(rows, axis=0).T
    both = turned[pl.ds(0, half, stride=2), :] + turned[pl.ds(1, half, stride=2), :]
    return both[:width, :width], both[:width, half : half + width]


def local_terms(grad, vals, pot, faces, penalty, orientation, diag, cross, scales, edge, grads, tiles, pots, sides,
                pens, codes, stage, turned, sems):
    comps, width, count, points = grad.shape
    even = points // LANES * LANES
    rows = width * count

    moves = [
        pltpu.make_async_copy(source, target, sems.at[comps + n])
        for n, (source, target) in enumerate(
            ((penalty, pens), (orientation, codes), (merged(faces), sides), (pot, pots), (merged(vals), tiles))
        )
    ]

    def grad_move(comp):
        return pltpu.make_async_copy(merged(grad).at[comp], grads.at[comp], sems.at[comp])

    for move in moves:
        move.start()
    for comp in range(comps):
        grad_move(comp).start()
    for move in moves[:3]:
        move.wait()

    first = lax.axis_index("elem") * count
    total = penalty.shape[0]
    row, col = parities(rows)

    def code_at(element):
        return codes[lax.rem(first + element, total)]

    def sign_of(code):
        return (1 - 2 * code).astype(jnp.float32)

    def pen_between(element):
        left = pens[lax.rem(first + element + total - 1, total)]
        return 0.5 * (left + pens[lax.rem(first + element, total)])

    uppers = [sides[element, 1 - code_at(element)] for element in range(count)]
    lowers = [sides[element, code_at(element)] for element in range(count)]

    def face_part(element):
        mixed = jnp.where(row != col, 0.25 * sign_of(code_at(element)), 0.0)
        both = row + col == 0
        upper_scale = jnp.where(both, pen_between(element + 1), -mixed)
        lower_scale = jnp.where(both, pen_between(element), mixed)
        upper, lower = uppers[element], lowers[element]
        return (upper_scale * gram(upper, upper) + lower_scale * gram(lower, lower)) * (1.0 / FP)

    def cross_scale(element):
        upper_sign, lower_sign = sign_of(code_at(element)), sign_of(code_at(element + 1))
        return (1.0 / FP) * jnp.where(
            row == 0,
            jnp.where(col == 0, -pen_between(element + 1), 0.25 * upper_sign),
            jnp.where(col == 0, -0.25 * lower_sign, 0.0),
        )

    cross[...] = cross_scale(0) * gram(lowers[1], uppers[0])
    edge[...] = uppers[count - 1]
    scale = cross_scale(count - 1)
    for side in range(2):
        scales[side] = jnp.where(code_at(count) == side, scale, 0.0)
    face_parts = [face_part(element) for element in range(count)]

    for move in moves[3:]:
        move.wait()
    odd = lax.broadcasted_iota(jnp.int32, (rows, LANES), 0) % 2 == 1

    def weighted(tile, level):
        level = jnp.where(odd[:, : tile.shape[1]], level[1:2], level[0:1])
        return (tile.astype(jnp.float32) * level * (1.0 / PTS)).astype(jnp.bfloat16)

    tile = tiles[:, :even]
    parts = [weighted(tile[:, at : at + LANES], pots[:, at : at + LANES]) for at in range(0, even, LANES)]
    end = tiles[:, even:]
    volume = gram(jnp.concatenate(parts, axis=1), tile) + gram(weighted(end, pots[:, even:]), end)

    masks = [(row == element) & (col == element) for element in range(count)]
    inner = 0.5 * (volume + volume.T)
    steady = [jnp.where(mask, inner, 0.0) + part for mask, part in zip(masks, face_parts)]

    def add_comp(comp, kinetic):
        grad_move(comp).wait()
        slope = grads[comp, :, :even]
        end = grads[comp, :, even:]
        return kinetic + gram(slope, slope) + gram(end, end)

    kinetic = lax.fori_loop(0, comps, add_comp, jnp.zeros((rows, rows), jnp.float32))
    parts = [part + jnp.where(mask, (0.5 / PTS) * kinetic, 0.0) for part, mask in zip(steady, masks)]
    diag[0], diag[1] = fold(*parts, stage, turned, width)


def pair_terms(arrived, edge, cross, scales, diag, out, stage, turned, rows):
    width = diag.shape[1]
    share = out.shape[2]
    upper = edge[...]
    parts = [gram(merged(arrived[0, side]), upper) * scales[side] for side in range(2)]
    pairs = fold(cross[...], parts[0] + parts[1], stage, turned, width)
    kinds = 2 * len(pairs)
    for element, pair in enumerate(pairs):
        rows[pl.ds(2 * element, width, stride=kinds), :] = diag[element]
        rows[pl.ds(2 * element + 1, width, stride=kinds), :] = pair
    ways = out.shape[0] // 2
    start = own_slots(ways)
    slots = [exchange_order(ways).index(owner) for owner in range(ways)]
    out[pl.ds(ways - start, ways)] = jnp.zeros((ways, kinds, share), jnp.float32)
    for owner in range(ways):
        at, end = owner * share, (owner + 1) * share
        pieces = []
        while at < end:
            row, col = divmod(at, width)
            size = min(width - col, end - at)
            pieces.append(rows[pl.ds(kinds * row, kinds), pl.ds(col, size)])
            at += size
        out[start + slots[owner]] = jnp.concatenate(pieces, axis=1)


def own_slots(ways):
    elem = lax.axis_index("elem")
    second = lax.rem(elem // 2, 4) // 2
    return ways * jnp.where((elem == 0) | (elem == 4), 1 - second, second)


def exchange_order(ways):
    rings = max(ways // 2, 1)
    root = 2 * (5 * rings // 8) + 1 if ways > 1 else 0

    def hops(share):
        step = (share // 2 - root // 2) % rings
        return min(step, rings - step) + 4 * ((share ^ root) & 1)

    return [root] + sorted((share for share in range(ways) if share != root), key=hops, reverse=True)


def exchange_groups(elems, ways):
    order = exchange_order(ways)
    return [
        [row * ways + share for row in ((elem, elem + 4) if elem else (4, 0)) for share in order]
        for elem in range(elems)
        if (elem // 2) % 4 < 2
    ]


def total_terms(shared, out):
    ways = shared.shape[0] // 2
    total = jnp.sum(shared[pl.ds(own_slots(ways), ways)], axis=0)
    for element in range(out.shape[0]):
        out[element] = total[2 * element : 2 * element + 2]


def from_behind(value, axis, steps):
    count = lax.axis_size(axis)
    pairs = [(source, (source + steps) % count) for source in range(count)]
    return lax.ppermute(value, axis, pairs)


def on_device(basis_vals, basis_grad, potential, face_traces, penalty, orientation):
    count, width, points = basis_vals.shape
    comps = basis_grad.shape[1]
    face_points = face_traces.shape[-1]
    faces = face_traces.transpose(0, 1, 3, 2, 4)
    arrived = from_behind(faces, "elem", -1)
    grad = basis_grad.transpose(1, 2, 0, 3)
    vals = basis_vals.transpose(1, 0, 2)
    held = (grad, vals, potential, faces, penalty, orientation)
    held = [pltpu.with_memory_space_constraint(array, pltpu.HBM) for array in held]
    rows = width * count
    any_space = pl.BlockSpec(memory_space=pl.ANY)
    in_vmem = pl.BlockSpec(memory_space=pltpu.VMEM)
    fold_scratch = [pltpu.VMEM((2, rows, rows), jnp.float32), pltpu.VMEM((rows, rows), jnp.float32)]
    diag, cross, scales, edge = pl.pallas_call(
        local_terms,
        out_shape=[
            pltpu.VMEM((count, width, width), jnp.float32),
            pltpu.VMEM((rows, rows), jnp.float32),
            pltpu.VMEM((2, rows, rows), jnp.float32),
            pltpu.VMEM((rows, face_points), jnp.bfloat16),
        ],
        in_specs=[any_space] * 6,
        out_specs=[in_vmem] * 4,
        scratch_shapes=[
            pltpu.VMEM((comps, rows, points), jnp.bfloat16),
            pltpu.VMEM((rows, points), jnp.bfloat16),
            pltpu.VMEM(potential.shape, jnp.float32),
            pltpu.VMEM((count, 2, rows, face_points), jnp.bfloat16),
            pltpu.SMEM(penalty.shape, jnp.float32),
            pltpu.SMEM(orientation.shape, jnp.int32),
            *fold_scratch,
            pltpu.SemaphoreType.DMA((comps + 5,)),
        ],
        compiler_params=pltpu.CompilerParams(vmem_limit_bytes=16 * MIB),
        cost_estimate=pl.CostEstimate(flops=400_000_000, bytes_accessed=3_000_000, transcendentals=0),
        name="local_terms",
    )(*held)
    ways = lax.axis_size("basis")
    share = width * width // ways
    terms = pl.pallas_call(
        pair_terms,
        out_shape=pltpu.VMEM((2 * ways, 2 * count, share), jnp.float32),
        in_specs=[in_vmem] * 5,
        out_specs=in_vmem,
        scratch_shapes=[*fold_scratch, pltpu.VMEM((2 * count * width, width), jnp.float32)],
        compiler_params=pltpu.CompilerParams(vmem_limit_bytes=8 * MIB),
        name="pair_terms",
    )(pltpu.with_memory_space_constraint(arrived, pltpu.VMEM), edge, cross, scales, diag)
    groups = exchange_groups(lax.axis_size("elem"), ways)
    shared = lax.all_to_all(terms, ("elem", "basis"), 0, 0, axis_index_groups=groups)
    return pl.pallas_call(
        total_terms,
        out_shape=jax.ShapeDtypeStruct((count, 2, share), jnp.float32),
        in_specs=[in_vmem],
        out_specs=in_vmem,
        compiler_params=pltpu.CompilerParams(vmem_limit_bytes=8 * MIB),
        name="total_terms",
    )(pltpu.with_memory_space_constraint(shared, pltpu.VMEM))


def solution(mesh):
    in_specs = (
        P("elem", None, "basis"),
        P("elem", None, None, "basis"),
        P("elem", "basis"),
        P("elem", None, None, None, "basis"),
        P(),
        P(),
    )
    out_specs = P("elem", None, "basis")
    return jax.shard_map(
        on_device, mesh=mesh, in_specs=in_specs, out_specs=out_specs, check_vma=False
    )
```

```python
import math

import jax
import jax.numpy as jnp
from jax import lax
from jax.experimental import pallas as pl
from jax.experimental.pallas import tpu as pltpu
from jax.sharding import PartitionSpec as P

PTS = 46656
FP = 1296
LANES = 128
NT = (((1,), (1,)), ((), ()))
MIB = 1024 * 1024


def gram(left, right):
    return lax.dot_general(left, right, NT, preferred_element_type=jnp.float32)


def merged(array):
    *lead, rows, pair, lanes = array.shape
    return array.reshape(*lead, rows * pair, lanes)


def parities(size):
    shape = (size, size)
    row = lax.broadcasted_iota(jnp.int32, shape, 0) % 2
    col = lax.broadcasted_iota(jnp.int32, shape, 1) % 2
    return row, col


def fold(matrices, stage, turned, width):
    size = matrices[0].shape[0]
    half = size // 2
    rows = []
    for n, matrix in enumerate(matrices):
        stage[n] = matrix
        rows.append(stage[n, pl.ds(0, half, stride=2), :] + stage[n, pl.ds(1, half, stride=2), :])
    wide = half * len(rows)
    turned[:, :wide] = jnp.concatenate(rows, axis=0).T
    both = turned[pl.ds(0, half, stride=2), :wide] + turned[pl.ds(1, half, stride=2), :wide]
    return [both[:width, n * half : n * half + width] for n in range(len(rows))]


def local_terms(grad, vals, pot, faces, penalty, orientation, chunks, scales, edge, grads, tiles, pots, sides,
                pens, codes, stage, turned, blocks, sems):
    comps, width, count, points = grad.shape
    even = points // LANES * LANES
    rows = width * count

    moves = [
        pltpu.make_async_copy(source, target, sems.at[comps + n])
        for n, (source, target) in enumerate(
            ((penalty, pens), (orientation, codes), (merged(faces), sides), (pot, pots), (merged(vals), tiles))
        )
    ]

    def grad_move(comp):
        return pltpu.make_async_copy(merged(grad).at[comp], grads.at[comp], sems.at[comp])

    for move in moves:
        move.start()
    for comp in range(comps):
        grad_move(comp).start()
    for move in moves[:3]:
        move.wait()

    first = lax.axis_index("elem") * count
    total = penalty.shape[0]
    row, col = parities(rows)

    def code_at(element):
        return codes[lax.rem(first + element, total)]

    def sign_of(code):
        return (1 - 2 * code).astype(jnp.float32)

    def pen_between(element):
        left = pens[lax.rem(first + element + total - 1, total)]
        return 0.5 * (left + pens[lax.rem(first + element, total)])

    uppers = [sides[element, 1 - code_at(element)] for element in range(count)]
    lowers = [sides[element, code_at(element)] for element in range(count)]

    def face_part(element):
        mixed = jnp.where(row != col, 0.25 * sign_of(code_at(element)), 0.0)
        both = row + col == 0
        upper_scale = jnp.where(both, pen_between(element + 1), -mixed)
        lower_scale = jnp.where(both, pen_between(element), mixed)
        upper, lower = uppers[element], lowers[element]
        return (upper_scale * gram(upper, upper) + lower_scale * gram(lower, lower)) * (1.0 / FP)

    def cross_scale(element):
        upper_sign, lower_sign = sign_of(code_at(element)), sign_of(code_at(element + 1))
        return (1.0 / FP) * jnp.where(
            row == 0,
            jnp.where(col == 0, -pen_between(element + 1), 0.25 * upper_sign),
            jnp.where(col == 0, -0.25 * lower_sign, 0.0),
        )

    (pair,) = fold([cross_scale(0) * gram(lowers[1], uppers[0])], stage, turned, width)
    kinds = 2 * count
    blocks[pl.ds(1, width, stride=kinds), :] = pair
    blocks[pl.ds(kinds - 1, width, stride=kinds), :] = jnp.zeros((width, width), jnp.float32)
    edge[...] = uppers[count - 1]
    scale = cross_scale(count - 1)
    for side in range(2):
        scales[side] = jnp.where(code_at(count) == side, scale, 0.0)
    face_parts = [face_part(element) for element in range(count)]

    for move in moves[3:]:
        move.wait()
    odd = lax.broadcasted_iota(jnp.int32, (rows, LANES), 0) % 2 == 1

    def weighted(tile, level):
        level = jnp.where(odd[:, : tile.shape[1]], level[1:2], level[0:1])
        return (tile.astype(jnp.float32) * level * (1.0 / PTS)).astype(jnp.bfloat16)

    tile = tiles[:, :even]
    parts = [weighted(tile[:, at : at + LANES], pots[:, at : at + LANES]) for at in range(0, even, LANES)]
    end = tiles[:, even:]
    volume = gram(jnp.concatenate(parts, axis=1), tile) + gram(weighted(end, pots[:, even:]), end)

    masks = [(row == element) & (col == element) for element in range(count)]
    inner = 0.5 * (volume + volume.T)
    steady = [jnp.where(mask, inner, 0.0) + part for mask, part in zip(masks, face_parts)]

    def add_comp(comp, kinetic):
        grad_move(comp).wait()
        slope = grads[comp, :, :even]
        end = grads[comp, :, even:]
        return kinetic + gram(slope, slope) + gram(end, end)

    kinetic = lax.fori_loop(0, comps, add_comp, jnp.zeros((rows, rows), jnp.float32))
    parts = [part + jnp.where(mask, (0.5 / PTS) * kinetic, 0.0) for part, mask in zip(steady, masks)]
    for element, diag in enumerate(fold(parts, stage, turned, width)):
        blocks[pl.ds(2 * element, width, stride=kinds), :] = diag

    share = chunks.shape[2]
    ways = chunks.shape[0] // 2
    start = own_slots(ways)
    chunks[pl.ds(ways - start, ways)] = jnp.zeros((ways, kinds, share), jnp.float32)
    for slot, owner in enumerate(exchange_order(ways)):
        pieces = [
            blocks[pl.ds(kinds * row, kinds), pl.ds(col, size)]
            for row, col, size in spans_of(owner * share, share, width)
        ]
        chunks[start + slot] = jnp.concatenate(pieces, axis=1)


def spans_of(at, share, width):
    end = at + share
    while at < end:
        row, col = divmod(at, width)
        size = min(width - col, end - at)
        yield row, col, size
        at += size


def pair_terms(arrived, edge, scales, chunks, out, stage, turned, rows):
    kinds, share = chunks.shape[1:]
    ways = chunks.shape[0] // 2
    width = rows.shape[0]
    upper = edge[...]
    parts = [gram(merged(arrived[0, side]), upper) * scales[side] for side in range(2)]
    (rows[...],) = fold([parts[0] + parts[1]], stage, turned, width)
    start = own_slots(ways)
    out[pl.ds(ways - start, ways)] = chunks[pl.ds(ways - start, ways)]
    order = exchange_order(ways)
    last = lax.broadcasted_iota(jnp.int32, (kinds, share), 0) == kinds - 1
    groups = math.gcd(ways, width)
    stride = width // groups
    for step in range(ways // groups):
        pieces = [
            rows[pl.ds(row, groups, stride=stride), :][:, col : col + size]
            for row, col, size in spans_of(step * share, share, width)
        ]
        added = jnp.concatenate(pieces, axis=1)
        for group in range(groups):
            slot = start + order.index(group * (ways // groups) + step)
            out[slot] = jnp.where(last, added[group : group + 1], chunks[slot])


def own_slots(ways):
    elem = lax.axis_index("elem")
    second = lax.rem(elem // 2, 4) // 2
    return ways * jnp.where((elem == 0) | (elem == 4), 1 - second, second)


def exchange_order(ways):
    rings = max(ways // 2, 1)
    root = 2 * (5 * rings // 8) + 1 if ways > 1 else 0

    def hops(share):
        step = (share // 2 - root // 2) % rings
        return min(step, rings - step) + 4 * ((share ^ root) & 1)

    return [root] + sorted((share for share in range(ways) if share != root), key=hops, reverse=True)


def exchange_groups(elems, ways):
    order = exchange_order(ways)
    return [
        [row * ways + share for row in ((elem, elem + 4) if elem else (4, 0)) for share in order]
        for elem in range(elems)
        if (elem // 2) % 4 < 2
    ]


def total_terms(shared, out):
    ways = shared.shape[0] // 2
    total = jnp.sum(shared[pl.ds(own_slots(ways), ways)], axis=0)
    for element in range(out.shape[0]):
        out[element] = total[2 * element : 2 * element + 2]


def from_behind(value, axis, steps):
    count = lax.axis_size(axis)
    pairs = [(source, (source + steps) % count) for source in range(count)]
    return lax.ppermute(value, axis, pairs)


def on_device(basis_vals, basis_grad, potential, face_traces, penalty, orientation):
    count, width, points = basis_vals.shape
    comps = basis_grad.shape[1]
    face_points = face_traces.shape[-1]
    faces = face_traces.transpose(0, 1, 3, 2, 4)
    arrived = from_behind(faces, "elem", -1)
    grad = basis_grad.transpose(1, 2, 0, 3)
    vals = basis_vals.transpose(1, 0, 2)
    held = (grad, vals, potential, faces, penalty, orientation)
    held = [pltpu.with_memory_space_constraint(array, pltpu.HBM) for array in held]
    rows = width * count
    any_space = pl.BlockSpec(memory_space=pl.ANY)
    in_vmem = pl.BlockSpec(memory_space=pltpu.VMEM)
    fold_scratch = [pltpu.VMEM((2, rows, rows), jnp.float32), pltpu.VMEM((rows, rows), jnp.float32)]
    ways = lax.axis_size("basis")
    share = width * width // ways
    terms = pltpu.VMEM((2 * ways, 2 * count, share), jnp.float32)
    chunks, scales, edge = pl.pallas_call(
        local_terms,
        out_shape=[
            terms,
            pltpu.VMEM((2, rows, rows), jnp.float32),
            pltpu.VMEM((rows, face_points), jnp.bfloat16),
        ],
        in_specs=[any_space] * 6,
        out_specs=[in_vmem] * 3,
        scratch_shapes=[
            pltpu.VMEM((comps, rows, points), jnp.bfloat16),
            pltpu.VMEM((rows, points), jnp.bfloat16),
            pltpu.VMEM(potential.shape, jnp.float32),
            pltpu.VMEM((count, 2, rows, face_points), jnp.bfloat16),
            pltpu.SMEM(penalty.shape, jnp.float32),
            pltpu.SMEM(orientation.shape, jnp.int32),
            *fold_scratch,
            pltpu.VMEM((2 * count * width, width), jnp.float32),
            pltpu.SemaphoreType.DMA((comps + 5,)),
        ],
        compiler_params=pltpu.CompilerParams(vmem_limit_bytes=16 * MIB),
        cost_estimate=pl.CostEstimate(flops=400_000_000, bytes_accessed=3_000_000, transcendentals=0),
        name="local_terms",
    )(*held)
    terms = pl.pallas_call(
        pair_terms,
        out_shape=terms,
        in_specs=[in_vmem] * 4,
        out_specs=in_vmem,
        scratch_shapes=[*fold_scratch, pltpu.VMEM((width, width), jnp.float32)],
        compiler_params=pltpu.CompilerParams(vmem_limit_bytes=8 * MIB),
        name="pair_terms",
    )(pltpu.with_memory_space_constraint(arrived, pltpu.VMEM), edge, scales, chunks)
    groups = exchange_groups(lax.axis_size("elem"), ways)
    shared = lax.all_to_all(terms, ("elem", "basis"), 0, 0, axis_index_groups=groups)
    return pl.pallas_call(
        total_terms,
        out_shape=jax.ShapeDtypeStruct((count, 2, share), jnp.float32),
        in_specs=[in_vmem],
        out_specs=in_vmem,
        compiler_params=pltpu.CompilerParams(vmem_limit_bytes=8 * MIB),
        name="total_terms",
    )(pltpu.with_memory_space_constraint(shared, pltpu.VMEM))


def solution(mesh):
    in_specs = (
        P("elem", None, "basis"),
        P("elem", None, None, "basis"),
        P("elem", "basis"),
        P("elem", None, None, None, "basis"),
        P(),
        P(),
    )
    out_specs = P("elem", None, "basis")
    return jax.shard_map(
        on_device, mesh=mesh, in_specs=in_specs, out_specs=out_specs, check_vma=False
    )
```

```python
import math

import jax
import jax.numpy as jnp
from jax import lax
from jax.experimental import pallas as pl
from jax.experimental.pallas import tpu as pltpu
from jax.sharding import PartitionSpec as P

PTS = 46656
FP = 1296
LANES = 128
NT = (((1,), (1,)), ((), ()))
MIB = 1024 * 1024


def gram(left, right):
    return lax.dot_general(left, right, NT, preferred_element_type=jnp.float32)


def merged(array):
    *lead, rows, pair, lanes = array.shape
    return array.reshape(*lead, rows * pair, lanes)


def parities(size):
    shape = (size, size)
    row = lax.broadcasted_iota(jnp.int32, shape, 0) % 2
    col = lax.broadcasted_iota(jnp.int32, shape, 1) % 2
    return row, col


def fold(matrices, stage, turned, width):
    size = matrices[0].shape[0]
    half = size // 2
    rows = []
    for n, matrix in enumerate(matrices):
        stage[n] = matrix
        rows.append(stage[n, pl.ds(0, half, stride=2), :] + stage[n, pl.ds(1, half, stride=2), :])
    wide = half * len(rows)
    turned[:, :wide] = jnp.concatenate(rows, axis=0).T
    both = turned[pl.ds(0, half, stride=2), :wide] + turned[pl.ds(1, half, stride=2), :wide]
    return [both[:width, n * half : n * half + width] for n in range(len(rows))]


def local_terms(grad, vals, pot, faces, penalty, orientation, chunks, scales, edge, grads, tiles, pots, sides,
                pens, codes, stage, turned, blocks, sems):
    comps, width, count, points = grad.shape
    even = points // LANES * LANES
    rows = width * count

    moves = [
        pltpu.make_async_copy(source, target, sems.at[comps + n])
        for n, (source, target) in enumerate(
            ((penalty, pens), (orientation, codes), (merged(faces), sides), (pot, pots), (merged(vals), tiles))
        )
    ]

    def grad_move(comp):
        return pltpu.make_async_copy(merged(grad).at[comp], grads.at[comp], sems.at[comp])

    for move in moves:
        move.start()
    for comp in range(comps):
        grad_move(comp).start()
    for move in moves[:3]:
        move.wait()

    first = lax.axis_index("elem") * count
    total = penalty.shape[0]
    row, col = parities(rows)

    def code_at(element):
        return codes[lax.rem(first + element, total)]

    def sign_of(code):
        return (1 - 2 * code).astype(jnp.float32)

    def pen_between(element):
        left = pens[lax.rem(first + element + total - 1, total)]
        return 0.5 * (left + pens[lax.rem(first + element, total)])

    uppers = [sides[element, 1 - code_at(element)] for element in range(count)]
    lowers = [sides[element, code_at(element)] for element in range(count)]

    def face_part(element):
        mixed = jnp.where(row != col, 0.25 * sign_of(code_at(element)), 0.0)
        both = row + col == 0
        upper_scale = jnp.where(both, pen_between(element + 1), -mixed)
        lower_scale = jnp.where(both, pen_between(element), mixed)
        upper, lower = uppers[element], lowers[element]
        return (upper_scale * gram(upper, upper) + lower_scale * gram(lower, lower)) * (1.0 / FP)

    def cross_scale(element):
        upper_sign, lower_sign = sign_of(code_at(element)), sign_of(code_at(element + 1))
        return (1.0 / FP) * jnp.where(
            row == 0,
            jnp.where(col == 0, -pen_between(element + 1), 0.25 * upper_sign),
            jnp.where(col == 0, -0.25 * lower_sign, 0.0),
        )

    (pair,) = fold([cross_scale(0) * gram(lowers[1], uppers[0])], stage, turned, width)
    kinds = 2 * count
    blocks[pl.ds(1, width, stride=kinds), :] = pair
    blocks[pl.ds(kinds - 1, width, stride=kinds), :] = jnp.zeros((width, width), jnp.float32)
    edge[...] = uppers[count - 1]
    scale = cross_scale(count - 1)
    for side in range(2):
        scales[side] = jnp.where(code_at(count) == side, scale, 0.0)
    face_parts = [face_part(element) for element in range(count)]

    for move in moves[3:]:
        move.wait()
    odd = lax.broadcasted_iota(jnp.int32, (rows, LANES), 0) % 2 == 1

    def weighted(tile, level):
        level = jnp.where(odd[:, : tile.shape[1]], level[1:2], level[0:1])
        return (tile.astype(jnp.float32) * level * (1.0 / PTS)).astype(jnp.bfloat16)

    tile = tiles[:, :even]
    parts = [weighted(tile[:, at : at + LANES], pots[:, at : at + LANES]) for at in range(0, even, LANES)]
    end = tiles[:, even:]
    volume = gram(jnp.concatenate(parts, axis=1), tile) + gram(weighted(end, pots[:, even:]), end)

    masks = [(row == element) & (col == element) for element in range(count)]
    inner = 0.5 * (volume + volume.T)
    steady = [jnp.where(mask, inner, 0.0) + part for mask, part in zip(masks, face_parts)]

    def add_comp(comp, kinetic):
        grad_move(comp).wait()
        slope = grads[comp, :, :even]
        end = grads[comp, :, even:]
        return kinetic + gram(slope, slope) + gram(end, end)

    kinetic = lax.fori_loop(0, comps, add_comp, jnp.zeros((rows, rows), jnp.float32))
    parts = [part + jnp.where(mask, (0.5 / PTS) * kinetic, 0.0) for part, mask in zip(steady, masks)]
    for element, diag in enumerate(fold(parts, stage, turned, width)):
        blocks[pl.ds(2 * element, width, stride=kinds), :] = diag

    share = chunks.shape[2]
    ways = chunks.shape[0] // 2
    start = own_slots(ways)
    chunks[pl.ds(ways - start, ways)] = jnp.zeros((ways, kinds, share), jnp.float32)
    for slot, owner in enumerate(exchange_order(ways)):
        pieces = [
            blocks[pl.ds(kinds * row, kinds), pl.ds(col, size)]
            for row, col, size in spans_of(owner * share, share, width)
        ]
        chunks[start + slot] = jnp.concatenate(pieces, axis=1)


def spans_of(at, share, width):
    end = at + share
    while at < end:
        row, col = divmod(at, width)
        size = min(width - col, end - at)
        yield row, col, size
        at += size


def pair_terms(arrived, edge, scales, chunks, out, stage, turned, rows):
    kinds, share = chunks.shape[1:]
    ways = chunks.shape[0] // 2
    width = rows.shape[0]
    upper = edge[...]
    parts = [gram(merged(arrived[0, side]), upper) * scales[side] for side in range(2)]
    (rows[...],) = fold([parts[0] + parts[1]], stage, turned, width)
    start = own_slots(ways)
    out[pl.ds(ways - start, ways)] = chunks[pl.ds(ways - start, ways)]
    order = exchange_order(ways)
    last = lax.broadcasted_iota(jnp.int32, (kinds, share), 0) == kinds - 1
    groups = math.gcd(ways, width)
    stride = width // groups
    for step in range(ways // groups):
        pieces = [
            rows[pl.ds(row, groups, stride=stride), :][:, col : col + size]
            for row, col, size in spans_of(step * share, share, width)
        ]
        added = jnp.concatenate(pieces, axis=1)
        for group in range(groups):
            slot = start + order.index(group * (ways // groups) + step)
            out[slot] = jnp.where(last, added[group : group + 1], chunks[slot])


def own_slots(ways):
    elem = lax.axis_index("elem")
    second = lax.rem(elem // 2, 4) // 2
    return ways * jnp.where((elem == 0) | (elem == 4), 1 - second, second)


def exchange_order(ways):
    rings = max(ways // 2, 1)
    root = 2 * (rings // 2) + 1 if ways > 1 else 0

    def hops(share):
        step = (share // 2 - root // 2) % rings
        return min(step, rings - step) + 4 * ((share ^ root) & 1)

    return [root] + sorted((share for share in range(ways) if share != root), key=hops, reverse=True)


def exchange_groups(elems, ways):
    order = exchange_order(ways)
    return [
        [row * ways + share for row in ((elem, elem + 4) if elem else (4, 0)) for share in order]
        for elem in range(elems)
        if (elem // 2) % 4 < 2
    ]


def total_terms(shared, out):
    ways = shared.shape[0] // 2
    total = jnp.sum(shared[pl.ds(own_slots(ways), ways)], axis=0)
    for element in range(out.shape[0]):
        out[element] = total[2 * element : 2 * element + 2]


def from_behind(value, axis, steps):
    count = lax.axis_size(axis)
    pairs = [(source, (source + steps) % count) for source in range(count)]
    return lax.ppermute(value, axis, pairs)


def on_device(basis_vals, basis_grad, potential, face_traces, penalty, orientation):
    count, width, points = basis_vals.shape
    comps = basis_grad.shape[1]
    face_points = face_traces.shape[-1]
    faces = face_traces.transpose(0, 1, 3, 2, 4)
    arrived = from_behind(faces, "elem", -1)
    grad = basis_grad.transpose(1, 2, 0, 3)
    vals = basis_vals.transpose(1, 0, 2)
    held = (grad, vals, potential, faces, penalty, orientation)
    held = [pltpu.with_memory_space_constraint(array, pltpu.HBM) for array in held]
    rows = width * count
    any_space = pl.BlockSpec(memory_space=pl.ANY)
    in_vmem = pl.BlockSpec(memory_space=pltpu.VMEM)
    fold_scratch = [pltpu.VMEM((2, rows, rows), jnp.float32), pltpu.VMEM((rows, rows), jnp.float32)]
    ways = lax.axis_size("basis")
    share = width * width // ways
    terms = pltpu.VMEM((2 * ways, 2 * count, share), jnp.float32)
    chunks, scales, edge = pl.pallas_call(
        local_terms,
        out_shape=[
            terms,
            pltpu.VMEM((2, rows, rows), jnp.float32),
            pltpu.VMEM((rows, face_points), jnp.bfloat16),
        ],
        in_specs=[any_space] * 6,
        out_specs=[in_vmem] * 3,
        scratch_shapes=[
            pltpu.VMEM((comps, rows, points), jnp.bfloat16),
            pltpu.VMEM((rows, points), jnp.bfloat16),
            pltpu.VMEM(potential.shape, jnp.float32),
            pltpu.VMEM((count, 2, rows, face_points), jnp.bfloat16),
            pltpu.SMEM(penalty.shape, jnp.float32),
            pltpu.SMEM(orientation.shape, jnp.int32),
            *fold_scratch,
            pltpu.VMEM((2 * count * width, width), jnp.float32),
            pltpu.SemaphoreType.DMA((comps + 5,)),
        ],
        compiler_params=pltpu.CompilerParams(vmem_limit_bytes=16 * MIB),
        cost_estimate=pl.CostEstimate(flops=400_000_000, bytes_accessed=3_000_000, transcendentals=0),
        name="local_terms",
    )(*held)
    terms = pl.pallas_call(
        pair_terms,
        out_shape=terms,
        in_specs=[in_vmem] * 4,
        out_specs=in_vmem,
        scratch_shapes=[*fold_scratch, pltpu.VMEM((width, width), jnp.float32)],
        compiler_params=pltpu.CompilerParams(vmem_limit_bytes=8 * MIB),
        name="pair_terms",
    )(pltpu.with_memory_space_constraint(arrived, pltpu.VMEM), edge, scales, chunks)
    groups = exchange_groups(lax.axis_size("elem"), ways)
    shared = lax.all_to_all(terms, ("elem", "basis"), 0, 0, axis_index_groups=groups)
    return pl.pallas_call(
        total_terms,
        out_shape=jax.ShapeDtypeStruct((count, 2, share), jnp.float32),
        in_specs=[in_vmem],
        out_specs=in_vmem,
        compiler_params=pltpu.CompilerParams(vmem_limit_bytes=8 * MIB),
        name="total_terms",
    )(pltpu.with_memory_space_constraint(shared, pltpu.VMEM))


def solution(mesh):
    in_specs = (
        P("elem", None, "basis"),
        P("elem", None, None, "basis"),
        P("elem", "basis"),
        P("elem", None, None, None, "basis"),
        P(),
        P(),
    )
    out_specs = P("elem", None, "basis")
    return jax.shard_map(
        on_device, mesh=mesh, in_specs=in_specs, out_specs=out_specs, check_vma=False
    )
```

```python
import math

import jax
import jax.numpy as jnp
from jax import lax
from jax.experimental import pallas as pl
from jax.experimental.pallas import tpu as pltpu
from jax.sharding import PartitionSpec as P

PTS = 46656
FP = 1296
LANES = 128
NT = (((1,), (1,)), ((), ()))
MIB = 1024 * 1024


def gram(left, right):
    return lax.dot_general(left, right, NT, preferred_element_type=jnp.float32)


def merged(array):
    *lead, rows, pair, lanes = array.shape
    return array.reshape(*lead, rows * pair, lanes)


def parities(size):
    shape = (size, size)
    row = lax.broadcasted_iota(jnp.int32, shape, 0) % 2
    col = lax.broadcasted_iota(jnp.int32, shape, 1) % 2
    return row, col


def fold(matrices, stage, turned, width):
    size = matrices[0].shape[0]
    half = size // 2
    rows = []
    for n, matrix in enumerate(matrices):
        stage[n] = matrix
        rows.append(stage[n, pl.ds(0, half, stride=2), :] + stage[n, pl.ds(1, half, stride=2), :])
    wide = half * len(rows)
    turned[:, :wide] = jnp.concatenate(rows, axis=0).T
    both = turned[pl.ds(0, half, stride=2), :wide] + turned[pl.ds(1, half, stride=2), :wide]
    return [both[:width, n * half : n * half + width] for n in range(len(rows))]


def local_terms(grad, vals, pot, faces, penalty, orientation, chunks, scales, edge, grads, tiles, pots, sides,
                pens, codes, stage, turned, blocks, sems):
    comps, width, count, points = grad.shape
    even = points // LANES * LANES
    rows = width * count

    moves = [
        pltpu.make_async_copy(source, target, sems.at[comps + n])
        for n, (source, target) in enumerate(
            ((penalty, pens), (orientation, codes), (merged(faces), sides), (pot, pots), (merged(vals), tiles))
        )
    ]

    def grad_move(comp):
        return pltpu.make_async_copy(merged(grad).at[comp], grads.at[comp], sems.at[comp])

    for move in moves:
        move.start()
    for comp in range(comps):
        grad_move(comp).start()
    for move in moves[:3]:
        move.wait()

    first = lax.axis_index("elem") * count
    total = penalty.shape[0]
    row, col = parities(rows)

    def code_at(element):
        return codes[lax.rem(first + element, total)]

    def sign_of(code):
        return (1 - 2 * code).astype(jnp.float32)

    def pen_between(element):
        left = pens[lax.rem(first + element + total - 1, total)]
        return 0.5 * (left + pens[lax.rem(first + element, total)])

    uppers = [sides[element, 1 - code_at(element)] for element in range(count)]
    lowers = [sides[element, code_at(element)] for element in range(count)]

    def face_part(element):
        mixed = jnp.where(row != col, 0.25 * sign_of(code_at(element)), 0.0)
        both = row + col == 0
        upper_scale = jnp.where(both, pen_between(element + 1), -mixed)
        lower_scale = jnp.where(both, pen_between(element), mixed)
        upper, lower = uppers[element], lowers[element]
        return (upper_scale * gram(upper, upper) + lower_scale * gram(lower, lower)) * (1.0 / FP)

    def cross_scale(element):
        upper_sign, lower_sign = sign_of(code_at(element)), sign_of(code_at(element + 1))
        return (1.0 / FP) * jnp.where(
            row == 0,
            jnp.where(col == 0, -pen_between(element + 1), 0.25 * upper_sign),
            jnp.where(col == 0, -0.25 * lower_sign, 0.0),
        )

    (pair,) = fold([cross_scale(0) * gram(lowers[1], uppers[0])], stage, turned, width)
    kinds = 2 * count
    blocks[pl.ds(1, width, stride=kinds), :] = pair
    blocks[pl.ds(kinds - 1, width, stride=kinds), :] = jnp.zeros((width, width), jnp.float32)
    edge[...] = uppers[count - 1]
    scale = cross_scale(count - 1)
    for side in range(2):
        scales[side] = jnp.where(code_at(count) == side, scale, 0.0)
    face_parts = [face_part(element) for element in range(count)]

    for move in moves[3:]:
        move.wait()
    odd = lax.broadcasted_iota(jnp.int32, (rows, LANES), 0) % 2 == 1

    def weighted(tile, level):
        level = jnp.where(odd[:, : tile.shape[1]], level[1:2], level[0:1])
        return (tile.astype(jnp.float32) * level * (1.0 / PTS)).astype(jnp.bfloat16)

    tile = tiles[:, :even]
    parts = [weighted(tile[:, at : at + LANES], pots[:, at : at + LANES]) for at in range(0, even, LANES)]
    end = tiles[:, even:]
    volume = gram(jnp.concatenate(parts, axis=1), tile) + gram(weighted(end, pots[:, even:]), end)

    masks = [(row == element) & (col == element) for element in range(count)]
    inner = 0.5 * (volume + volume.T)
    steady = [jnp.where(mask, inner, 0.0) + part for mask, part in zip(masks, face_parts)]

    def add_comp(comp, kinetic):
        grad_move(comp).wait()
        slope = grads[comp, :, :even]
        end = grads[comp, :, even:]
        return kinetic + gram(slope, slope) + gram(end, end)

    kinetic = jnp.zeros((rows, rows), jnp.float32)
    for comp in range(comps):
        kinetic = add_comp(comp, kinetic)
    parts = [part + jnp.where(mask, (0.5 / PTS) * kinetic, 0.0) for part, mask in zip(steady, masks)]
    for element, diag in enumerate(fold(parts, stage, turned, width)):
        blocks[pl.ds(2 * element, width, stride=kinds), :] = diag

    share = chunks.shape[2]
    ways = chunks.shape[0] // 2
    start = own_slots(ways)
    chunks[pl.ds(ways - start, ways)] = jnp.zeros((ways, kinds, share), jnp.float32)
    for slot, owner in enumerate(exchange_order(ways)):
        pieces = [
            blocks[pl.ds(kinds * row, kinds), pl.ds(col, size)]
            for row, col, size in spans_of(owner * share, share, width)
        ]
        chunks[start + slot] = jnp.concatenate(pieces, axis=1)


def spans_of(at, share, width):
    end = at + share
    while at < end:
        row, col = divmod(at, width)
        size = min(width - col, end - at)
        yield row, col, size
        at += size


def pair_terms(arrived, edge, scales, chunks, out, stage, turned, rows):
    kinds, share = chunks.shape[1:]
    ways = chunks.shape[0] // 2
    width = rows.shape[0]
    upper = edge[...]
    parts = [gram(merged(arrived[0, side]), upper) * scales[side] for side in range(2)]
    (rows[...],) = fold([parts[0] + parts[1]], stage, turned, width)
    start = own_slots(ways)
    out[pl.ds(ways - start, ways)] = chunks[pl.ds(ways - start, ways)]
    order = exchange_order(ways)
    last = lax.broadcasted_iota(jnp.int32, (kinds, share), 0) == kinds - 1
    groups = math.gcd(ways, width)
    stride = width // groups
    for step in range(ways // groups):
        pieces = [
            rows[pl.ds(row, groups, stride=stride), :][:, col : col + size]
            for row, col, size in spans_of(step * share, share, width)
        ]
        added = jnp.concatenate(pieces, axis=1)
        for group in range(groups):
            slot = start + order.index(group * (ways // groups) + step)
            out[slot] = jnp.where(last, added[group : group + 1], chunks[slot])


def own_slots(ways):
    elem = lax.axis_index("elem")
    second = lax.rem(elem // 2, 4) // 2
    return ways * jnp.where((elem == 0) | (elem == 4), 1 - second, second)


def exchange_order(ways):
    rings = max(ways // 2, 1)
    root = 2 * (5 * rings // 8) + 1 if ways > 1 else 0

    def hops(share):
        step = (share // 2 - root // 2) % rings
        return min(step, rings - step) + 4 * ((share ^ root) & 1)

    return [root] + sorted((share for share in range(ways) if share != root), key=hops, reverse=True)


def exchange_groups(elems, ways):
    order = exchange_order(ways)
    return [
        [row * ways + share for row in ((elem, elem + 4) if elem else (4, 0)) for share in order]
        for elem in range(elems)
        if (elem // 2) % 4 < 2
    ]


def total_terms(shared, out):
    ways = shared.shape[0] // 2
    total = jnp.sum(shared[pl.ds(own_slots(ways), ways)], axis=0)
    for element in range(out.shape[0]):
        out[element] = total[2 * element : 2 * element + 2]


def from_behind(value, axis, steps):
    count = lax.axis_size(axis)
    pairs = [(source, (source + steps) % count) for source in range(count)]
    return lax.ppermute(value, axis, pairs)


def on_device(basis_vals, basis_grad, potential, face_traces, penalty, orientation):
    count, width, points = basis_vals.shape
    comps = basis_grad.shape[1]
    face_points = face_traces.shape[-1]
    faces = face_traces.transpose(0, 1, 3, 2, 4)
    arrived = from_behind(faces, "elem", -1)
    grad = basis_grad.transpose(1, 2, 0, 3)
    vals = basis_vals.transpose(1, 0, 2)
    held = (grad, vals, potential, faces, penalty, orientation)
    held = [pltpu.with_memory_space_constraint(array, pltpu.HBM) for array in held]
    rows = width * count
    any_space = pl.BlockSpec(memory_space=pl.ANY)
    in_vmem = pl.BlockSpec(memory_space=pltpu.VMEM)
    fold_scratch = [pltpu.VMEM((2, rows, rows), jnp.float32), pltpu.VMEM((rows, rows), jnp.float32)]
    ways = lax.axis_size("basis")
    share = width * width // ways
    terms = pltpu.VMEM((2 * ways, 2 * count, share), jnp.float32)
    chunks, scales, edge = pl.pallas_call(
        local_terms,
        out_shape=[
            terms,
            pltpu.VMEM((2, rows, rows), jnp.float32),
            pltpu.VMEM((rows, face_points), jnp.bfloat16),
        ],
        in_specs=[any_space] * 6,
        out_specs=[in_vmem] * 3,
        scratch_shapes=[
            pltpu.VMEM((comps, rows, points), jnp.bfloat16),
            pltpu.VMEM((rows, points), jnp.bfloat16),
            pltpu.VMEM(potential.shape, jnp.float32),
            pltpu.VMEM((count, 2, rows, face_points), jnp.bfloat16),
            pltpu.SMEM(penalty.shape, jnp.float32),
            pltpu.SMEM(orientation.shape, jnp.int32),
            *fold_scratch,
            pltpu.VMEM((2 * count * width, width), jnp.float32),
            pltpu.SemaphoreType.DMA((comps + 5,)),
        ],
        compiler_params=pltpu.CompilerParams(vmem_limit_bytes=16 * MIB),
        cost_estimate=pl.CostEstimate(flops=400_000_000, bytes_accessed=3_000_000, transcendentals=0),
        name="local_terms",
    )(*held)
    terms = pl.pallas_call(
        pair_terms,
        out_shape=terms,
        in_specs=[in_vmem] * 4,
        out_specs=in_vmem,
        scratch_shapes=[*fold_scratch, pltpu.VMEM((width, width), jnp.float32)],
        compiler_params=pltpu.CompilerParams(vmem_limit_bytes=8 * MIB),
        name="pair_terms",
    )(pltpu.with_memory_space_constraint(arrived, pltpu.VMEM), edge, scales, chunks)
    groups = exchange_groups(lax.axis_size("elem"), ways)
    shared = lax.all_to_all(terms, ("elem", "basis"), 0, 0, axis_index_groups=groups)
    return pl.pallas_call(
        total_terms,
        out_shape=jax.ShapeDtypeStruct((count, 2, share), jnp.float32),
        in_specs=[in_vmem],
        out_specs=in_vmem,
        compiler_params=pltpu.CompilerParams(vmem_limit_bytes=8 * MIB),
        name="total_terms",
    )(pltpu.with_memory_space_constraint(shared, pltpu.VMEM))


def solution(mesh):
    in_specs = (
        P("elem", None, "basis"),
        P("elem", None, None, "basis"),
        P("elem", "basis"),
        P("elem", None, None, None, "basis"),
        P(),
        P(),
    )
    out_specs = P("elem", None, "basis")
    return jax.shard_map(
        on_device, mesh=mesh, in_specs=in_specs, out_specs=out_specs, check_vma=False
    )
```

```python
import math

import jax
import jax.numpy as jnp
from jax import lax
from jax.experimental import pallas as pl
from jax.experimental.pallas import tpu as pltpu
from jax.sharding import PartitionSpec as P

PTS = 46656
FP = 1296
LANES = 128
NT = (((1,), (1,)), ((), ()))
MIB = 1024 * 1024


def gram(left, right):
    return lax.dot_general(left, right, NT, preferred_element_type=jnp.float32)


def merged(array):
    *lead, rows, pair, lanes = array.shape
    return array.reshape(*lead, rows * pair, lanes)


def parities(size):
    shape = (size, size)
    row = lax.broadcasted_iota(jnp.int32, shape, 0) % 2
    col = lax.broadcasted_iota(jnp.int32, shape, 1) % 2
    return row, col


def fold(matrices, stage, turned, width):
    size = matrices[0].shape[0]
    half = size // 2
    rows = []
    for n, matrix in enumerate(matrices):
        stage[n] = matrix
        rows.append(stage[n, pl.ds(0, half, stride=2), :] + stage[n, pl.ds(1, half, stride=2), :])
    wide = half * len(rows)
    turned[:, :wide] = jnp.concatenate(rows, axis=0).T
    both = turned[pl.ds(0, half, stride=2), :wide] + turned[pl.ds(1, half, stride=2), :wide]
    return [both[:width, n * half : n * half + width] for n in range(len(rows))]


def local_terms(grad, vals, pot, faces, penalty, orientation, chunks, scales, edge, grads, tiles, pots, sides,
                pens, codes, stage, turned, blocks, lefts, sems):
    comps, width, count, points = grad.shape
    even = points // LANES * LANES
    rows = width * count

    moves = [
        pltpu.make_async_copy(source, target, sems.at[comps + n])
        for n, (source, target) in enumerate(
            ((penalty, pens), (orientation, codes), (merged(faces), sides), (pot, pots), (merged(vals), tiles))
        )
    ]

    def grad_move(comp):
        return pltpu.make_async_copy(merged(grad).at[comp], grads.at[comp], sems.at[comp])

    for move in moves:
        move.start()
    for comp in range(comps):
        grad_move(comp).start()
    for move in moves[:3]:
        move.wait()

    first = lax.axis_index("elem") * count
    total = penalty.shape[0]
    row, col = parities(rows)

    def code_at(element):
        return codes[lax.rem(first + element, total)]

    def sign_of(code):
        return (1 - 2 * code).astype(jnp.float32)

    def pen_between(element):
        left = pens[lax.rem(first + element + total - 1, total)]
        return 0.5 * (left + pens[lax.rem(first + element, total)])

    uppers = [sides[element, 1 - code_at(element)] for element in range(count)]
    lowers = [sides[element, code_at(element)] for element in range(count)]

    def face_part(element):
        mixed = jnp.where(row != col, 0.25 * sign_of(code_at(element)), 0.0)
        both = row + col == 0
        upper_scale = jnp.where(both, pen_between(element + 1), -mixed)
        lower_scale = jnp.where(both, pen_between(element), mixed)
        upper, lower = uppers[element], lowers[element]
        return (upper_scale * gram(upper, upper) + lower_scale * gram(lower, lower)) * (1.0 / FP)

    def cross_scale(element):
        upper_sign, lower_sign = sign_of(code_at(element)), sign_of(code_at(element + 1))
        return (1.0 / FP) * jnp.where(
            row == 0,
            jnp.where(col == 0, -pen_between(element + 1), 0.25 * upper_sign),
            jnp.where(col == 0, -0.25 * lower_sign, 0.0),
        )

    (pair,) = fold([cross_scale(0) * gram(lowers[1], uppers[0])], stage, turned, width)
    kinds = 2 * count
    blocks[pl.ds(1, width, stride=kinds), :] = pair
    blocks[pl.ds(kinds - 1, width, stride=kinds), :] = jnp.zeros((width, width), jnp.float32)
    edge[...] = uppers[count - 1]
    scale = cross_scale(count - 1)
    for side in range(2):
        scales[side] = jnp.where(code_at(count) == side, scale, 0.0)
    face_parts = [face_part(element) for element in range(count)]

    for move in moves[3:]:
        move.wait()
    odd = lax.broadcasted_iota(jnp.int32, (rows, LANES), 0) % 2 == 1

    def weighted(tile, level):
        level = jnp.where(odd[:, : tile.shape[1]], level[1:2], level[0:1])
        return (tile.astype(jnp.float32) * level * (1.0 / PTS)).astype(jnp.bfloat16)

    def weigh(step, carry):
        lanes = pl.ds(pl.multiple_of(step * LANES, LANES), LANES)
        lefts[:, lanes] = weighted(tiles[:, lanes], pots[:, lanes])
        return carry

    lax.fori_loop(0, even // LANES, weigh, 0)
    end = tiles[:, even:]
    volume = gram(lefts[...], tiles[:, :even]) + gram(weighted(end, pots[:, even:]), end)

    masks = [(row == element) & (col == element) for element in range(count)]
    inner = 0.5 * (volume + volume.T)
    steady = [jnp.where(mask, inner, 0.0) + part for mask, part in zip(masks, face_parts)]

    def add_comp(comp, kinetic):
        grad_move(comp).wait()
        slope = grads[comp, :, :even]
        end = grads[comp, :, even:]
        return kinetic + gram(slope, slope) + gram(end, end)

    kinetic = lax.fori_loop(0, comps, add_comp, jnp.zeros((rows, rows), jnp.float32))
    parts = [part + jnp.where(mask, (0.5 / PTS) * kinetic, 0.0) for part, mask in zip(steady, masks)]
    for element, diag in enumerate(fold(parts, stage, turned, width)):
        blocks[pl.ds(2 * element, width, stride=kinds), :] = diag

    share = chunks.shape[2]
    ways = chunks.shape[0] // 2
    start = own_slots(ways)
    chunks[pl.ds(ways - start, ways)] = jnp.zeros((ways, kinds, share), jnp.float32)
    for slot, owner in enumerate(exchange_order(ways)):
        pieces = [
            blocks[pl.ds(kinds * row, kinds), pl.ds(col, size)]
            for row, col, size in spans_of(owner * share, share, width)
        ]
        chunks[start + slot] = jnp.concatenate(pieces, axis=1)


def spans_of(at, share, width):
    end = at + share
    while at < end:
        row, col = divmod(at, width)
        size = min(width - col, end - at)
        yield row, col, size
        at += size


def pair_terms(arrived, edge, scales, chunks, out, stage, turned, rows):
    kinds, share = chunks.shape[1:]
    ways = chunks.shape[0] // 2
    width = rows.shape[0]
    upper = edge[...]
    parts = [gram(merged(arrived[0, side]), upper) * scales[side] for side in range(2)]
    (rows[...],) = fold([parts[0] + parts[1]], stage, turned, width)
    start = own_slots(ways)
    out[pl.ds(ways - start, ways)] = chunks[pl.ds(ways - start, ways)]
    order = exchange_order(ways)
    last = lax.broadcasted_iota(jnp.int32, (kinds, share), 0) == kinds - 1
    groups = math.gcd(ways, width)
    stride = width // groups
    for step in range(ways // groups):
        pieces = [
            rows[pl.ds(row, groups, stride=stride), :][:, col : col + size]
            for row, col, size in spans_of(step * share, share, width)
        ]
        added = jnp.concatenate(pieces, axis=1)
        for group in range(groups):
            slot = start + order.index(group * (ways // groups) + step)
            out[slot] = jnp.where(last, added[group : group + 1], chunks[slot])


def own_slots(ways):
    elem = lax.axis_index("elem")
    second = lax.rem(elem // 2, 4) // 2
    return ways * jnp.where((elem == 0) | (elem == 4), 1 - second, second)


def exchange_order(ways):
    rings = max(ways // 2, 1)
    root = 2 * (5 * rings // 8) + 1 if ways > 1 else 0

    def hops(share):
        step = (share // 2 - root // 2) % rings
        return min(step, rings - step) + 4 * ((share ^ root) & 1)

    return [root] + sorted((share for share in range(ways) if share != root), key=hops, reverse=True)


def exchange_groups(elems, ways):
    order = exchange_order(ways)
    return [
        [row * ways + share for row in ((elem, elem + 4) if elem else (4, 0)) for share in order]
        for elem in range(elems)
        if (elem // 2) % 4 < 2
    ]


def total_terms(shared, out):
    ways = shared.shape[0] // 2
    total = jnp.sum(shared[pl.ds(own_slots(ways), ways)], axis=0)
    for element in range(out.shape[0]):
        out[element] = total[2 * element : 2 * element + 2]


def from_behind(value, axis, steps):
    count = lax.axis_size(axis)
    pairs = [(source, (source + steps) % count) for source in range(count)]
    return lax.ppermute(value, axis, pairs)


def on_device(basis_vals, basis_grad, potential, face_traces, penalty, orientation):
    count, width, points = basis_vals.shape
    comps = basis_grad.shape[1]
    face_points = face_traces.shape[-1]
    faces = face_traces.transpose(0, 1, 3, 2, 4)
    arrived = from_behind(faces, "elem", -1)
    grad = basis_grad.transpose(1, 2, 0, 3)
    vals = basis_vals.transpose(1, 0, 2)
    held = (grad, vals, potential, faces, penalty, orientation)
    held = [pltpu.with_memory_space_constraint(array, pltpu.HBM) for array in held]
    rows = width * count
    any_space = pl.BlockSpec(memory_space=pl.ANY)
    in_vmem = pl.BlockSpec(memory_space=pltpu.VMEM)
    fold_scratch = [pltpu.VMEM((2, rows, rows), jnp.float32), pltpu.VMEM((rows, rows), jnp.float32)]
    ways = lax.axis_size("basis")
    share = width * width // ways
    terms = pltpu.VMEM((2 * ways, 2 * count, share), jnp.float32)
    chunks, scales, edge = pl.pallas_call(
        local_terms,
        out_shape=[
            terms,
            pltpu.VMEM((2, rows, rows), jnp.float32),
            pltpu.VMEM((rows, face_points), jnp.bfloat16),
        ],
        in_specs=[any_space] * 6,
        out_specs=[in_vmem] * 3,
        scratch_shapes=[
            pltpu.VMEM((comps, rows, points), jnp.bfloat16),
            pltpu.VMEM((rows, points), jnp.bfloat16),
            pltpu.VMEM(potential.shape, jnp.float32),
            pltpu.VMEM((count, 2, rows, face_points), jnp.bfloat16),
            pltpu.SMEM(penalty.shape, jnp.float32),
            pltpu.SMEM(orientation.shape, jnp.int32),
            *fold_scratch,
            pltpu.VMEM((2 * count * width, width), jnp.float32),
            pltpu.VMEM((rows, points // LANES * LANES), jnp.bfloat16),
            pltpu.SemaphoreType.DMA((comps + 5,)),
        ],
        compiler_params=pltpu.CompilerParams(vmem_limit_bytes=16 * MIB),
        cost_estimate=pl.CostEstimate(flops=400_000_000, bytes_accessed=3_000_000, transcendentals=0),
        name="local_terms",
    )(*held)
    terms = pl.pallas_call(
        pair_terms,
        out_shape=terms,
        in_specs=[in_vmem] * 4,
        out_specs=in_vmem,
        scratch_shapes=[*fold_scratch, pltpu.VMEM((width, width), jnp.float32)],
        compiler_params=pltpu.CompilerParams(vmem_limit_bytes=8 * MIB),
        name="pair_terms",
    )(pltpu.with_memory_space_constraint(arrived, pltpu.VMEM), edge, scales, chunks)
    groups = exchange_groups(lax.axis_size("elem"), ways)
    shared = lax.all_to_all(terms, ("elem", "basis"), 0, 0, axis_index_groups=groups)
    return pl.pallas_call(
        total_terms,
        out_shape=jax.ShapeDtypeStruct((count, 2, share), jnp.float32),
        in_specs=[in_vmem],
        out_specs=in_vmem,
        compiler_params=pltpu.CompilerParams(vmem_limit_bytes=8 * MIB),
        name="total_terms",
    )(pltpu.with_memory_space_constraint(shared, pltpu.VMEM))


def solution(mesh):
    in_specs = (
        P("elem", None, "basis"),
        P("elem", None, None, "basis"),
        P("elem", "basis"),
        P("elem", None, None, None, "basis"),
        P(),
        P(),
    )
    out_specs = P("elem", None, "basis")
    return jax.shard_map(
        on_device, mesh=mesh, in_specs=in_specs, out_specs=out_specs, check_vma=False
    )
```

```python
import math

import jax
import jax.numpy as jnp
from jax import lax
from jax.experimental import pallas as pl
from jax.experimental.pallas import tpu as pltpu
from jax.sharding import PartitionSpec as P

PTS = 46656
FP = 1296
LANES = 128
NT = (((1,), (1,)), ((), ()))
MIB = 1024 * 1024


def gram(left, right):
    return lax.dot_general(left, right, NT, preferred_element_type=jnp.float32)


def merged(array):
    *lead, rows, pair, lanes = array.shape
    return array.reshape(*lead, rows * pair, lanes)


def parities(size):
    shape = (size, size)
    row = lax.broadcasted_iota(jnp.int32, shape, 0) % 2
    col = lax.broadcasted_iota(jnp.int32, shape, 1) % 2
    return row, col


def fold(matrices, stage, turned, width):
    size = matrices[0].shape[0]
    half = size // 2
    rows = []
    for n, matrix in enumerate(matrices):
        stage[n] = matrix
        rows.append(stage[n, pl.ds(0, half, stride=2), :] + stage[n, pl.ds(1, half, stride=2), :])
    wide = half * len(rows)
    turned[:, :wide] = jnp.concatenate(rows, axis=0).T
    both = turned[pl.ds(0, half, stride=2), :wide] + turned[pl.ds(1, half, stride=2), :wide]
    return [both[:width, n * half : n * half + width] for n in range(len(rows))]


def local_terms(grad, vals, pot, faces, penalty, orientation, chunks, scales, edge, grads, tiles, pots, sides,
                pens, codes, stage, turned, blocks, sems):
    comps, width, count, points = grad.shape
    even = points // LANES * LANES
    rows = width * count

    moves = [
        pltpu.make_async_copy(source, target, sems.at[comps + n])
        for n, (source, target) in enumerate(
            ((penalty, pens), (orientation, codes), (merged(faces), sides), (pot, pots), (merged(vals), tiles))
        )
    ]

    grad_move = pltpu.make_async_copy(merged(grad), grads, sems.at[0])

    for move in moves:
        move.start()
    grad_move.start()
    for move in moves[:3]:
        move.wait()

    first = lax.axis_index("elem") * count
    total = penalty.shape[0]
    row, col = parities(rows)

    def code_at(element):
        return codes[lax.rem(first + element, total)]

    def sign_of(code):
        return (1 - 2 * code).astype(jnp.float32)

    def pen_between(element):
        left = pens[lax.rem(first + element + total - 1, total)]
        return 0.5 * (left + pens[lax.rem(first + element, total)])

    uppers = [sides[element, 1 - code_at(element)] for element in range(count)]
    lowers = [sides[element, code_at(element)] for element in range(count)]

    def face_part(element):
        mixed = jnp.where(row != col, 0.25 * sign_of(code_at(element)), 0.0)
        both = row + col == 0
        upper_scale = jnp.where(both, pen_between(element + 1), -mixed)
        lower_scale = jnp.where(both, pen_between(element), mixed)
        upper, lower = uppers[element], lowers[element]
        return (upper_scale * gram(upper, upper) + lower_scale * gram(lower, lower)) * (1.0 / FP)

    def cross_scale(element):
        upper_sign, lower_sign = sign_of(code_at(element)), sign_of(code_at(element + 1))
        return (1.0 / FP) * jnp.where(
            row == 0,
            jnp.where(col == 0, -pen_between(element + 1), 0.25 * upper_sign),
            jnp.where(col == 0, -0.25 * lower_sign, 0.0),
        )

    (pair,) = fold([cross_scale(0) * gram(lowers[1], uppers[0])], stage, turned, width)
    kinds = 2 * count
    blocks[pl.ds(1, width, stride=kinds), :] = pair
    blocks[pl.ds(kinds - 1, width, stride=kinds), :] = jnp.zeros((width, width), jnp.float32)
    edge[...] = uppers[count - 1]
    scale = cross_scale(count - 1)
    for side in range(2):
        scales[side] = jnp.where(code_at(count) == side, scale, 0.0)
    face_parts = [face_part(element) for element in range(count)]

    for move in moves[3:]:
        move.wait()
    odd = lax.broadcasted_iota(jnp.int32, (rows, LANES), 0) % 2 == 1

    def weighted(tile, level):
        level = jnp.where(odd[:, : tile.shape[1]], level[1:2], level[0:1])
        return (tile.astype(jnp.float32) * level * (1.0 / PTS)).astype(jnp.bfloat16)

    tile = tiles[:, :even]
    parts = [weighted(tile[:, at : at + LANES], pots[:, at : at + LANES]) for at in range(0, even, LANES)]
    end = tiles[:, even:]
    volume = gram(jnp.concatenate(parts, axis=1), tile) + gram(weighted(end, pots[:, even:]), end)

    masks = [(row == element) & (col == element) for element in range(count)]
    inner = 0.5 * (volume + volume.T)
    steady = [jnp.where(mask, inner, 0.0) + part for mask, part in zip(masks, face_parts)]

    def add_comp(comp, kinetic):
        slope = grads[comp, :, :even]
        end = grads[comp, :, even:]
        return kinetic + gram(slope, slope) + gram(end, end)

    grad_move.wait()
    kinetic = lax.fori_loop(0, comps, add_comp, jnp.zeros((rows, rows), jnp.float32))
    parts = [part + jnp.where(mask, (0.5 / PTS) * kinetic, 0.0) for part, mask in zip(steady, masks)]
    for element, diag in enumerate(fold(parts, stage, turned, width)):
        blocks[pl.ds(2 * element, width, stride=kinds), :] = diag

    share = chunks.shape[2]
    ways = chunks.shape[0] // 2
    start = own_slots(ways)
    chunks[pl.ds(ways - start, ways)] = jnp.zeros((ways, kinds, share), jnp.float32)
    for slot, owner in enumerate(exchange_order(ways)):
        pieces = [
            blocks[pl.ds(kinds * row, kinds), pl.ds(col, size)]
            for row, col, size in spans_of(owner * share, share, width)
        ]
        chunks[start + slot] = jnp.concatenate(pieces, axis=1)


def spans_of(at, share, width):
    end = at + share
    while at < end:
        row, col = divmod(at, width)
        size = min(width - col, end - at)
        yield row, col, size
        at += size


def pair_terms(arrived, edge, scales, chunks, out, stage, turned, rows):
    kinds, share = chunks.shape[1:]
    ways = chunks.shape[0] // 2
    width = rows.shape[0]
    upper = edge[...]
    parts = [gram(merged(arrived[0, side]), upper) * scales[side] for side in range(2)]
    (rows[...],) = fold([parts[0] + parts[1]], stage, turned, width)
    start = own_slots(ways)
    out[pl.ds(ways - start, ways)] = chunks[pl.ds(ways - start, ways)]
    order = exchange_order(ways)
    last = lax.broadcasted_iota(jnp.int32, (kinds, share), 0) == kinds - 1
    groups = math.gcd(ways, width)
    stride = width // groups
    for step in range(ways // groups):
        pieces = [
            rows[pl.ds(row, groups, stride=stride), :][:, col : col + size]
            for row, col, size in spans_of(step * share, share, width)
        ]
        added = jnp.concatenate(pieces, axis=1)
        for group in range(groups):
            slot = start + order.index(group * (ways // groups) + step)
            out[slot] = jnp.where(last, added[group : group + 1], chunks[slot])


def own_slots(ways):
    elem = lax.axis_index("elem")
    second = lax.rem(elem // 2, 4) // 2
    return ways * jnp.where((elem == 0) | (elem == 4), 1 - second, second)


def exchange_order(ways):
    rings = max(ways // 2, 1)
    root = 2 * (5 * rings // 8) + 1 if ways > 1 else 0

    def hops(share):
        step = (share // 2 - root // 2) % rings
        return min(step, rings - step) + 4 * ((share ^ root) & 1)

    return [root] + sorted((share for share in range(ways) if share != root), key=hops, reverse=True)


def exchange_groups(elems, ways):
    order = exchange_order(ways)
    return [
        [row * ways + share for row in ((elem, elem + 4) if elem else (4, 0)) for share in order]
        for elem in range(elems)
        if (elem // 2) % 4 < 2
    ]


def total_terms(shared, out):
    ways = shared.shape[0] // 2
    total = jnp.sum(shared[pl.ds(own_slots(ways), ways)], axis=0)
    for element in range(out.shape[0]):
        out[element] = total[2 * element : 2 * element + 2]


def from_behind(value, axis, steps):
    count = lax.axis_size(axis)
    pairs = [(source, (source + steps) % count) for source in range(count)]
    return lax.ppermute(value, axis, pairs)


def on_device(basis_vals, basis_grad, potential, face_traces, penalty, orientation):
    count, width, points = basis_vals.shape
    comps = basis_grad.shape[1]
    face_points = face_traces.shape[-1]
    faces = face_traces.transpose(0, 1, 3, 2, 4)
    arrived = from_behind(faces, "elem", -1)
    grad = basis_grad.transpose(1, 2, 0, 3)
    vals = basis_vals.transpose(1, 0, 2)
    held = (grad, vals, potential, faces, penalty, orientation)
    held = [pltpu.with_memory_space_constraint(array, pltpu.HBM) for array in held]
    rows = width * count
    any_space = pl.BlockSpec(memory_space=pl.ANY)
    in_vmem = pl.BlockSpec(memory_space=pltpu.VMEM)
    fold_scratch = [pltpu.VMEM((2, rows, rows), jnp.float32), pltpu.VMEM((rows, rows), jnp.float32)]
    ways = lax.axis_size("basis")
    share = width * width // ways
    terms = pltpu.VMEM((2 * ways, 2 * count, share), jnp.float32)
    chunks, scales, edge = pl.pallas_call(
        local_terms,
        out_shape=[
            terms,
            pltpu.VMEM((2, rows, rows), jnp.float32),
            pltpu.VMEM((rows, face_points), jnp.bfloat16),
        ],
        in_specs=[any_space] * 6,
        out_specs=[in_vmem] * 3,
        scratch_shapes=[
            pltpu.VMEM((comps, rows, points), jnp.bfloat16),
            pltpu.VMEM((rows, points), jnp.bfloat16),
            pltpu.VMEM(potential.shape, jnp.float32),
            pltpu.VMEM((count, 2, rows, face_points), jnp.bfloat16),
            pltpu.SMEM(penalty.shape, jnp.float32),
            pltpu.SMEM(orientation.shape, jnp.int32),
            *fold_scratch,
            pltpu.VMEM((2 * count * width, width), jnp.float32),
            pltpu.SemaphoreType.DMA((comps + 5,)),
        ],
        compiler_params=pltpu.CompilerParams(vmem_limit_bytes=16 * MIB),
        cost_estimate=pl.CostEstimate(flops=400_000_000, bytes_accessed=3_000_000, transcendentals=0),
        name="local_terms",
    )(*held)
    terms = pl.pallas_call(
        pair_terms,
        out_shape=terms,
        in_specs=[in_vmem] * 4,
        out_specs=in_vmem,
        scratch_shapes=[*fold_scratch, pltpu.VMEM((width, width), jnp.float32)],
        compiler_params=pltpu.CompilerParams(vmem_limit_bytes=8 * MIB),
        name="pair_terms",
    )(pltpu.with_memory_space_constraint(arrived, pltpu.VMEM), edge, scales, chunks)
    groups = exchange_groups(lax.axis_size("elem"), ways)
    shared = lax.all_to_all(terms, ("elem", "basis"), 0, 0, axis_index_groups=groups)
    return pl.pallas_call(
        total_terms,
        out_shape=jax.ShapeDtypeStruct((count, 2, share), jnp.float32),
        in_specs=[in_vmem],
        out_specs=in_vmem,
        compiler_params=pltpu.CompilerParams(vmem_limit_bytes=8 * MIB),
        name="total_terms",
    )(pltpu.with_memory_space_constraint(shared, pltpu.VMEM))


def solution(mesh):
    in_specs = (
        P("elem", None, "basis"),
        P("elem", None, None, "basis"),
        P("elem", "basis"),
        P("elem", None, None, None, "basis"),
        P(),
        P(),
    )
    out_specs = P("elem", None, "basis")
    return jax.shard_map(
        on_device, mesh=mesh, in_specs=in_specs, out_specs=out_specs, check_vma=False
    )
```
